32 devices in a mesh: prompt: 8 (over z, x), seq: 4 (over y, core).
Axes of the slice: x: 2, y: 2, z: 4, core: 2. Of those that a mesh axis runs over, the one named last changes fastest.
Arguments:
- queries: bfloat16 [8, 2048, 1024], P('prompt', 'seq'), may hold values from -5 to 5
- resp_kv: bfloat16 [8, 2048, 256], P('prompt', 'seq'), may hold values from -16 to 16
- prefix_kv: bfloat16 [8, 192, 256], P('prompt', 'seq'), may hold values from -16 to 16
- lengths: int32 [8, 4], P('prompt'), may hold values from 256 to 512, as said below
- upstream: bfloat16 [8, 2048, 1024], P('prompt', 'seq'), may hold values from -6 to 6
Outputs:
- attended: bfloat16 [8, 2048, 1024], P('prompt', 'seq')
- grad_queries: bfloat16 [8, 2048, 1024], P('prompt', 'seq')
- grad_resp_kv: float32 [8, 2048, 256], P('prompt', 'seq')
- grad_prefix_kv: float32 [8, 192, 256], P('prompt', 'seq')
The draws below stay inside these ranges and needn't reach their ends.
Inputs may be any that keep to these rules, and one draw needn't show every extreme that they name: `lengths`: each prompt's 4 responses fill its slots in order from slot 0; one response of every prompt has exactly 512 tokens.
All inputs are finite; a program needn't handle non-finite values.
Results may differ from the reference program's by a relative error of at most 0.011.
Values may be sent and summed in bfloat16 or wider, within the bound.
A program may use at most 192 MiB of HBM per device.

```python
import jax
import jax.numpy as jnp
from jax import lax

HQ = 8
DH = 128
LMAX = 512
PROMPTS = 8
NRESP = 4
SLOTS = 2048
PREFIX = 192
N_SEQ = 4


def draw_queries(key, part):
    key = jax.random.fold_in(key, 11)
    base = jnp.clip(jax.random.normal(key, (PROMPTS, SLOTS, HQ * DH), jnp.float32), -4.0, 4.0)
    return base.astype(jnp.bfloat16)


def draw_prefix_kv(key, part):
    key = jax.random.fold_in(key, 12)
    key_keys, key_values = jax.random.split(key)
    key_part = jnp.clip(jax.random.normal(key_keys, (PROMPTS, PREFIX, DH), jnp.float32), -4.0, 4.0)
    value_part = 4.0 * jnp.clip(jax.random.normal(key_values, (PROMPTS, PREFIX, DH), jnp.float32), -4.0, 4.0)
    return jnp.concatenate([key_part, value_part], axis=-1).astype(jnp.bfloat16)


def draw_resp_kv(key, part):
    key = jax.random.fold_in(key, 13)
    key_keys, key_values = jax.random.split(key)
    key_part = jnp.clip(jax.random.normal(key_keys, (PROMPTS, SLOTS, DH), jnp.float32), -4.0, 4.0)
    value_part = 4.0 * jnp.clip(jax.random.normal(key_values, (PROMPTS, SLOTS, DH), jnp.float32), -4.0, 4.0)
    return jnp.concatenate([key_part, value_part], axis=-1).astype(jnp.bfloat16)


def draw_lengths(key, part):
    key = jax.random.fold_in(key, 14)
    key_base, key_place = jax.random.split(key)
    base = jax.random.randint(key_base, (PROMPTS, NRESP), LMAX // 2, LMAX + 1)
    place = jax.random.randint(key_place, (PROMPTS,), 0, NRESP)
    chosen = jnp.arange(NRESP, dtype=jnp.int32)[None, :] == place[:, None]
    return jnp.where(chosen, LMAX, base).astype(jnp.int32)


def block_levels(key, shape, cuts, low, top_value):
    def one(dim, shards_of):
        heights = jax.random.uniform(jax.random.fold_in(jax.random.fold_in(key, 6), dim), (shards_of,), jnp.float32, low / len(cuts), top_value / len(cuts))
        return jnp.repeat(jnp.exp(heights), shape[dim] // shards_of).reshape((-1,) + (1,) * (len(shape) - dim - 1))

    factor_of = one(*cuts[0])
    for cut in cuts[1:]:
        factor_of = factor_of * one(*cut)
    return factor_of


def scatter_about(rng, dims, width, bound, cuts=(), kind=jnp.bfloat16):
    values = width * jax.random.normal(rng, dims, jnp.float32)
    if cuts:
        values = values * block_levels(rng, dims, cuts, -0.22, 0.18)
    return jnp.clip(values, -bound, bound).astype(kind)


def setup_inputs(seed: int = 0) -> dict:
    key_list = jax.random.split(jax.random.key(seed), 6)
    return {
        "queries": draw_queries(jax.random.fold_in(key_list[5], 71), 0),
        "resp_kv": draw_resp_kv(jax.random.fold_in(key_list[5], 71), 0),
        "prefix_kv": draw_prefix_kv(jax.random.fold_in(key_list[5], 71), 0),
        "lengths": draw_lengths(jax.random.fold_in(key_list[5], 71), 0),
        "upstream": scatter_about(key_list[4], (PROMPTS, SLOTS, HQ * DH), 1.0, 6.0, ((0, 8), (1, 4))),
    }


def rounded(values):
    return lax.optimization_barrier(values.astype(jnp.bfloat16)).astype(jnp.float32)


def slot_segments(resp_ends, slot_ids):
    counted = jnp.sum((slot_ids[:, None] >= resp_ends[None, :]).astype(jnp.int32), axis=1)
    return jnp.where(slot_ids < 0, -1, counted).astype(jnp.int32)


def shard_terms(query_rows, key_vals, visible, live_rows, upstream_rows, factor):
    head_dim = query_rows.shape[-1]
    score_scale = head_dim ** -0.5
    key_part = key_vals[:, :head_dim].astype(jnp.float32)
    value_part = key_vals[:, head_dim:].astype(jnp.float32)
    query_f = query_rows.astype(jnp.float32)
    scores = jnp.einsum('rhd,kd->rhk', query_f, key_part) * score_scale
    scores = jnp.where(visible[:, None, :], scores, -jnp.inf)
    row_max = jnp.max(scores, axis=-1, keepdims=True)
    weights = jnp.exp(scores - row_max)
    row_total = jnp.sum(weights, axis=-1, keepdims=True)
    mixed = jnp.einsum('rhk,kd->rhd', rounded(weights), value_part) / row_total
    attended = (mixed * live_rows[:, None, None]).astype(jnp.bfloat16)
    log_total = row_max + jnp.log(row_total)
    grad_out = rounded(upstream_rows.astype(jnp.float32) * factor * live_rows[:, None, None])
    delta = jnp.sum(grad_out * attended.astype(jnp.float32), axis=-1, keepdims=True)
    probs = jnp.exp(scores - log_total)
    dprobs = jnp.einsum('rhd,kd->rhk', grad_out, value_part)
    dscores = rounded(probs * (dprobs - delta))
    probs_low = rounded(probs)
    grad_query = (jnp.einsum('rhk,kd->rhd', dscores, key_part) * score_scale).astype(jnp.bfloat16)
    key_grads = jnp.einsum('rhk,rhd->kd', dscores, query_f) * score_scale
    value_grads = jnp.einsum('rhk,rhd->kd', probs_low, grad_out)
    return attended, grad_query, jnp.concatenate([key_grads, value_grads], axis=1)


def reference(queries, resp_kv, prefix_kv, lengths, upstream):
    factor = jnp.float32(PROMPTS * SLOTS) / jnp.sum(lengths).astype(jnp.float32)

    def one_prompt(items):
        query_all, kv_all, prefix_all, length_row, upstream_all = items
        resp_ends = jnp.cumsum(length_row).astype(jnp.int32)
        query_four = query_all.reshape(N_SEQ, LMAX, HQ, DH)
        upstream_four = upstream_all.reshape(N_SEQ, LMAX, HQ, DH)
        kv_three = kv_all.reshape(N_SEQ, LMAX, 2 * DH)
        earlier = jnp.concatenate([jnp.zeros((1, LMAX, 2 * DH), kv_all.dtype), kv_three[:-1]], axis=0)

        def step(carry, inputs):
            query_rows, upstream_rows, own_kv, prev_kv, shard_index = inputs
            positions = shard_index * LMAX + jnp.arange(LMAX, dtype=jnp.int32)
            own_seg = slot_segments(resp_ends, positions)
            prev_seg = slot_segments(resp_ends, positions - LMAX)
            live_rows = (own_seg < NRESP).astype(jnp.float32)
            key_slots = jnp.concatenate([positions - LMAX, positions])
            key_segs = jnp.concatenate([prev_seg, own_seg])
            same_resp = (key_segs[None, :] == own_seg[:, None]) & (key_slots[None, :] <= positions[:, None])
            visible = jnp.concatenate([jnp.ones((LMAX, PREFIX), jnp.bool_), same_resp], axis=1)
            key_vals = jnp.concatenate([prefix_all, prev_kv, own_kv], axis=0)
            attended, grad_query, kv_grads = shard_terms(query_rows, key_vals, visible, live_rows, upstream_rows, factor)
            carry = carry + kv_grads[:PREFIX]
            return carry, (attended, grad_query, kv_grads[PREFIX:PREFIX + LMAX], kv_grads[PREFIX + LMAX:])

        start = jnp.zeros((PREFIX, 2 * DH), jnp.float32)
        prefix_grads, stacked = lax.scan(step, start, (query_four, upstream_four, kv_three, earlier, jnp.arange(N_SEQ, dtype=jnp.int32)))
        attended, grad_query, prev_grads, own_grads = stacked
        later = jnp.concatenate([prev_grads[1:], jnp.zeros((1, LMAX, 2 * DH), jnp.float32)], axis=0)
        resp_grads = own_grads + later
        return (attended.reshape(SLOTS, HQ * DH), grad_query.reshape(SLOTS, HQ * DH), resp_grads.reshape(SLOTS, 2 * DH), prefix_grads)

    attended, grad_queries, grad_resp_kv, grad_prefix_kv = lax.map(one_prompt, (queries, resp_kv, prefix_kv, lengths, upstream))
    return (attended, grad_queries, grad_resp_kv, grad_prefix_kv)
```

```python
import functools
import math

import jax
import jax.numpy as jnp
from jax import lax
from jax.experimental import pallas as pl
from jax.experimental.pallas import tpu as pltpu
from jax.sharding import PartitionSpec as P

F32 = jnp.float32
BF16 = jnp.bfloat16
TILE = 128
HIDDEN = -1e30
PAIR = 2
ONES = 16


def mm(a, b):
    return lax.dot_general(a, b, (((1,), (0,)), ((), ())), preferred_element_type=F32)


def mm_nt(a, b):
    return lax.dot_general(a, b, (((1,), (1,)), ((), ())), preferred_element_type=F32)


def kernel(
    n_prompt,
    n_seq,
    lens_ref,
    q_hbm,
    kv_hbm,
    pkv_hbm,
    up_hbm,
    att_hbm,
    gq_hbm,
    gkv_hbm,
    gpf_hbm,
    q_ref,
    up_ref,
    win,
    pfx,
    win_kt,
    win_vt,
    pfx_kt,
    pfx_vt,
    bias,
    att,
    gq,
    acc,
    acc_p,
    ret_out,
    ret_in,
    gp_out,
    gp_in,
    gkv,
    gpf,
    lens_all,
    in_sem,
    out_sem,
    pf_send,
    pf_recv,
    prev_send,
    prev_recv,
    len_send,
    len_recv,
    ret_send,
    ret_recv,
    gp_send,
    gp_recv,
):
    rows = q_ref.shape[0]
    dim = win.shape[1] // 2
    heads = q_ref.shape[1] // dim
    tiles = rows // TILE
    block = pkv_hbm.shape[1]
    span = rows + TILE
    responses = lens_ref.shape[1]
    scale = dim ** (-0.5)
    my_p = lax.axis_index("prompt")
    me = lax.axis_index("seq")
    has_next = me < n_seq - 1
    has_prev = me > 0

    seq_peers = [lax.rem(me + d, n_seq) for d in range(1, n_seq)]
    prompt_peers = [lax.rem(my_p + d, n_prompt) for d in range(1, n_prompt)]

    barrier = pltpu.get_barrier_semaphore()
    for peer in seq_peers:
        pl.semaphore_signal(
            barrier, inc=1, device_id=(my_p, peer), device_id_type=pl.DeviceIdType.MESH
        )
    for peer in prompt_peers:
        pl.semaphore_signal(
            barrier, inc=1, device_id=(peer, me), device_id_type=pl.DeviceIdType.MESH
        )

    own_block = pl.ds(pl.multiple_of(me * block, 16), block)
    loads = [
        pltpu.make_async_copy(kv_hbm.at[0], win.at[pl.ds(rows, rows)], in_sem.at[0]),
        pltpu.make_async_copy(pkv_hbm.at[0], pfx.at[own_block], in_sem.at[1]),
        pltpu.make_async_copy(q_hbm.at[0], q_ref, in_sem.at[2]),
        pltpu.make_async_copy(up_hbm.at[0], up_ref, in_sem.at[3]),
    ]
    for load in loads:
        load.start()

    total = lens_ref[0, 0]
    for r in range(1, responses):
        total = total + lens_ref[0, r]
    lens_all[my_p] = jnp.full((8, 128), total, jnp.int32).astype(F32)

    pl.semaphore_wait(barrier, n_seq - 1 + n_prompt - 1)

    def remote(src, dst, send, recv, target):
        return pltpu.make_async_remote_copy(
            src_ref=src,
            dst_ref=dst,
            send_sem=send,
            recv_sem=recv,
            device_id=target,
            device_id_type=pl.DeviceIdType.MESH,
        )

    def part(j):
        return pl.ds(j * TILE, TILE)

    def prev_copy(j):
        return remote(
            kv_hbm.at[0, part(j)],
            win.at[part(j)],
            prev_send.at[j],
            prev_recv.at[j],
            (my_p, me + 1),
        )

    def ret_copy(j):
        return remote(
            ret_out.at[part(j)],
            ret_in.at[part(j)],
            ret_send.at[j],
            ret_recv.at[j],
            (my_p, me - 1),
        )

    def pf_copy(d, sender, target):
        rows_of = pl.ds(pl.multiple_of(sender * block, 16), block)
        return remote(
            pkv_hbm.at[0], pfx.at[rows_of], pf_send.at[d], pf_recv.at[sender], (my_p, target)
        )

    def len_copy(d, sender, target):
        return remote(
            lens_all.at[sender],
            lens_all.at[sender],
            len_send.at[d],
            len_recv.at[sender],
            (target, me),
        )

    def gp_copy(d, sender, target):
        rows_of = pl.ds(pl.multiple_of(target * block, 16), block)
        return remote(
            gp_out.at[rows_of],
            gp_in.at[sender],
            gp_send.at[d],
            gp_recv.at[sender],
            (my_p, target),
        )

    order = [tiles - 1] + list(range(tiles - 1))
    for d, peer in enumerate(seq_peers):
        pf_copy(d, me, peer).start()

    @pl.when(has_next)
    def _():
        prev_copy(order[0]).start()

    for d, peer in enumerate(prompt_peers):
        len_copy(d, my_p, peer).start()

    @pl.when(has_next)
    def _():
        for j in order[1:]:
            prev_copy(j).start()

    @pl.when(jnp.logical_not(has_prev))
    def _():
        win[pl.ds(0, rows)] = jnp.zeros((rows, 2 * dim), BF16)

    @pl.when(jnp.logical_not(has_next))
    def _():
        ret_in[...] = jnp.zeros((rows, 2 * dim), BF16)

    acc[...] = jnp.zeros_like(acc)
    acc_p[...] = jnp.zeros_like(acc_p)
    win_vt[pl.ds(dim, ONES)] = jnp.ones((ONES, 2 * rows), BF16)
    pfx_vt[pl.ds(dim, ONES)] = jnp.ones((ONES, pfx.shape[0]), BF16)

    def turn(j):
        keys = win[part(j), :dim]
        values = win[part(j), dim:]
        win_kt[:, part(j)] = keys.T
        win_vt[pl.ds(0, dim), part(j)] = values.T

    loads[0].wait()
    for j in range(tiles, 2 * tiles):
        turn(j)
    for load in loads[1:]:
        load.wait()
    for d, peer in enumerate(seq_peers):
        pf_copy(d, peer, me).wait_recv()
    pfx_kt[...] = pfx[:, :dim].T
    pfx_vt[pl.ds(0, dim)] = pfx[:, dim:].T

    @pl.when(has_prev)
    def _():
        prev_copy(order[0]).wait_recv()

    turn(order[0])
    for d, peer in enumerate(prompt_peers):
        len_copy(d, peer, my_p).wait_recv()
    tokens = lens_all[0]
    for p in range(1, n_prompt):
        tokens = tokens + lens_all[p]
    factor = (F32(n_prompt * n_seq * rows) / tokens)[:1]
    factor2 = jnp.concatenate([factor] * PAIR, axis=1)

    def out_copies(i):
        return (
            pltpu.make_async_copy(
                att.at[part(i)], att_hbm.at[0, part(i)], out_sem.at[2 * i]
            ),
            pltpu.make_async_copy(
                gq.at[part(i)], gq_hbm.at[0, part(i)], out_sem.at[2 * i + 1]
            ),
        )

    def tile_step(i):
        start_row = pl.multiple_of(i * TILE, TILE)
        own = pl.ds(start_row, TILE)
        window = pl.ds(start_row, span)

        slots = me * rows + start_row + lax.broadcasted_iota(jnp.int32, (1, TILE), 1)
        first = jnp.zeros((1, TILE), jnp.int32)
        end = jnp.int32(0)
        for r in range(responses):
            end = end + lens_ref[0, r]
            first = jnp.where(slots >= end, end, first)
        live = jnp.where(slots < end, F32(1), F32(0))
        live2 = jnp.concatenate([live] * PAIR, axis=1)
        key_slots = (me - 1) * rows + start_row + lax.broadcasted_iota(jnp.int32, (span, TILE), 0)
        seen = (key_slots >= first) & (key_slots <= slots)
        one_bias = jnp.where(seen, F32(0), F32(HIDDEN))
        for k in range(PAIR):
            bias[:, pl.ds(k * TILE, TILE)] = one_bias

        k_w = win[window, :dim]
        v_w = win[window, dim:]
        k_p = pfx[:, :dim]
        v_p = pfx[:, dim:]
        kt_w = win_kt[:, window]
        vt_w = win_vt[:, window]

        q_parts, g_parts = [], []
        wp_parts, ww_parts, sp_parts, sw_parts = [], [], [], []
        for pair in range(heads // PAIR):
            cols = [pl.ds((pair * PAIR + k) * dim, dim) for k in range(PAIR)]
            q2 = jnp.concatenate([q_ref[own, c] for c in cols], axis=0)
            up_t = jnp.concatenate([up_ref[own, c].T for c in cols], axis=1)
            s_p = mm_nt(k_p, q2)
            s_w = mm_nt(k_w, q2) + bias[...]
            top = jnp.maximum(
                jnp.max(s_p, axis=0, keepdims=True), jnp.max(s_w, axis=0, keepdims=True)
            )
            step = scale * math.log2(math.e)
            w_p = jnp.exp2((s_p - top) * step).astype(BF16)
            w_w = jnp.exp2((s_w - top) * step).astype(BF16)
            mixed = mm(pfx_vt[...], w_p) + mm(vt_w, w_w)
            inverse = live2 / mixed[dim : dim + 1]
            att_t = (mixed[:dim] * inverse).astype(BF16)
            g_t = (up_t.astype(F32) * inverse).astype(BF16)
            delta = jnp.sum(g_t.astype(F32) * att_t.astype(F32), axis=0, keepdims=True)
            d_p = (w_p.astype(F32) * (mm(v_p, g_t) - delta)).astype(BF16)
            d_w = (w_w.astype(F32) * (mm(v_w, g_t) - delta)).astype(BF16)
            gq_t = ((mm(pfx_kt[...], d_p) + mm(kt_w, d_w)) * (factor2 * scale)).astype(BF16)
            for k, c in enumerate(cols):
                att[own, c] = att_t[:, k * TILE : (k + 1) * TILE].T
                gq[own, c] = gq_t[:, k * TILE : (k + 1) * TILE].T
            q_parts.append(q2)
            g_parts.append(g_t)
            wp_parts.append(w_p)
            ww_parts.append(w_w)
            sp_parts.append(d_p)
            sw_parts.append(d_w)
        q_all = jnp.concatenate(q_parts, axis=0)
        g_all = jnp.concatenate(g_parts, axis=1)
        acc_p[:, :dim] += mm(jnp.concatenate(sp_parts, axis=1), q_all)
        acc[window, :dim] += mm(jnp.concatenate(sw_parts, axis=1), q_all)
        acc_p[:, dim:] += mm_nt(jnp.concatenate(wp_parts, axis=1), g_all)
        acc[window, dim:] += mm_nt(jnp.concatenate(ww_parts, axis=1), g_all)

    def give_back(j):
        ret_out[part(j)] = acc[part(j)].astype(BF16)

        @pl.when(has_prev)
        def _():
            ret_copy(j).start()

    def round_step(s, carry):
        i = lax.rem(s + tiles - 1, tiles)

        @pl.when(s == 1)
        def _():
            @pl.when(has_prev)
            def _():
                for j in order[1:]:
                    prev_copy(j).wait_recv()

            for j in order[1:]:
                turn(j)

        tile_step(i)
        for copy in out_copies(i):
            copy.start()
        for k in range(1, tiles - 1):

            @pl.when(s == k)
            def _():
                give_back(k - 1)

        return carry

    lax.fori_loop(0, tiles, round_step, 0)

    gp_out[...] = acc_p[...].astype(BF16)
    for d, peer in enumerate(seq_peers):
        gp_copy(d, me, peer).start()
    for j in (tiles - 2, tiles - 1):
        give_back(j)

    final = jnp.concatenate([factor * scale, factor], axis=1)
    for j in range(tiles):

        @pl.when(has_next)
        def _():
            pltpu.make_async_remote_copy(
                src_ref=ret_out.at[part(j)],
                dst_ref=ret_in.at[part(j)],
                send_sem=ret_send.at[j],
                recv_sem=ret_recv.at[j],
                device_id=(my_p, me + 1),
                device_id_type=pl.DeviceIdType.MESH,
            ).wait_recv()

        gkv[part(j)] = (acc[part(tiles + j)] + ret_in[part(j)].astype(F32)) * final
    gkv_copy = pltpu.make_async_copy(gkv, gkv_hbm.at[0], out_sem.at[2 * tiles])
    gkv_copy.start()

    sums = acc_p[own_block]
    for d, peer in enumerate(seq_peers):
        gp_copy(d, peer, me).wait_recv()
        sums = sums + gp_in[peer].astype(F32)
    gpf[...] = sums * final
    gpf_copy = pltpu.make_async_copy(gpf, gpf_hbm.at[0], out_sem.at[2 * tiles + 1])
    gpf_copy.start()

    for d, peer in enumerate(seq_peers):
        pf_copy(d, me, peer).wait_send()
        gp_copy(d, me, peer).wait_send()
    for d, peer in enumerate(prompt_peers):
        len_copy(d, my_p, peer).wait_send()

    @pl.when(has_next)
    def _():
        for j in order:
            prev_copy(j).wait_send()

    @pl.when(has_prev)
    def _():
        for j in range(tiles):
            ret_copy(j).wait_send()

    for i in range(tiles):
        for copy in out_copies(i):
            copy.wait()
    gkv_copy.wait()
    gpf_copy.wait()


def body(n_prompt, n_seq, queries, resp_kv, prefix_kv, lengths, upstream):
    rows, width = queries.shape[1:]
    dim = resp_kv.shape[2] // 2
    block = prefix_kv.shape[1]
    prefix = block * n_seq
    tiles = rows // TILE
    dma = pltpu.SemaphoreType.DMA
    anywhere = pl.BlockSpec(memory_space=pl.ANY)
    vmem = pltpu.VMEM
    return pl.pallas_call(
        functools.partial(kernel, n_prompt, n_seq),
        out_shape=(
            jax.ShapeDtypeStruct(queries.shape, BF16),
            jax.ShapeDtypeStruct(queries.shape, BF16),
            jax.ShapeDtypeStruct(resp_kv.shape, F32),
            jax.ShapeDtypeStruct(prefix_kv.shape, F32),
        ),
        in_specs=[pl.BlockSpec(memory_space=pltpu.SMEM)] + [anywhere] * 4,
        out_specs=(anywhere,) * 4,
        scratch_shapes=[
            vmem((rows, width), BF16),
            vmem((rows, width), BF16),
            vmem((2 * rows, 2 * dim), BF16),
            vmem((prefix, 2 * dim), BF16),
            vmem((dim, 2 * rows), BF16),
            vmem((dim + ONES, 2 * rows), BF16),
            vmem((dim, prefix), BF16),
            vmem((dim + ONES, prefix), BF16),
            vmem((rows + TILE, PAIR * TILE), F32),
            vmem((rows, width), BF16),
            vmem((rows, width), BF16),
            vmem((2 * rows, 2 * dim), F32),
            vmem((prefix, 2 * dim), F32),
            vmem((rows, 2 * dim), BF16),
            vmem((rows, 2 * dim), BF16),
            vmem((prefix, 2 * dim), BF16),
            vmem((n_seq, block, 2 * dim), BF16),
            vmem((rows, 2 * dim), F32),
            vmem((block, 2 * dim), F32),
            vmem((n_prompt, 8, 128), F32),
            dma((4,)),
            dma((2 * tiles + 2,)),
            dma((n_seq,)),
            dma((n_seq,)),
            dma((tiles,)),
            dma((tiles,)),
            dma((n_prompt,)),
            dma((n_prompt,)),
            dma((tiles,)),
            dma((tiles,)),
            dma((n_seq,)),
            dma((n_seq,)),
        ],
        compiler_params=pltpu.CompilerParams(
            collective_id=0, has_side_effects=True, vmem_limit_bytes=50 * 1024 * 1024
        ),
        name="attention_core",
    )(lengths, queries, resp_kv, prefix_kv, upstream)


def solution(mesh):
    spec = P("prompt", "seq", None)
    return jax.shard_map(
        functools.partial(body, mesh.shape["prompt"], mesh.shape["seq"]),
        mesh=mesh,
        in_specs=(spec, spec, spec, P("prompt", None), spec),
        out_specs=(spec, spec, spec, spec),
        check_vma=False,
    )
```

```python
import functools
import math

import jax
import jax.numpy as jnp
from jax import lax
from jax.experimental import pallas as pl
from jax.experimental.pallas import tpu as pltpu
from jax.sharding import PartitionSpec as P

F32 = jnp.float32
BF16 = jnp.bfloat16
TILE = 128
HIDDEN = -1e30
PAIR = 2
ONES = 16


def mm(a, b):
    return lax.dot_general(a, b, (((1,), (0,)), ((), ())), preferred_element_type=F32)


def mm_nt(a, b):
    return lax.dot_general(a, b, (((1,), (1,)), ((), ())), preferred_element_type=F32)


def kernel(
    n_prompt,
    n_seq,
    lens_ref,
    q_hbm,
    kv_hbm,
    pkv_hbm,
    up_hbm,
    att_hbm,
    gq_hbm,
    gkv_hbm,
    gpf_hbm,
    q_ref,
    up_ref,
    win,
    pfx,
    win_kt,
    win_vt,
    pfx_kt,
    pfx_vt,
    bias,
    s_ref,
    w_ref,
    d_ref,
    att,
    gq,
    acc,
    acc_p,
    ret_out,
    ret_in,
    gp_out,
    gp_in,
    gkv,
    gpf,
    lens_all,
    in_sem,
    out_sem,
    pf_send,
    pf_recv,
    prev_send,
    prev_recv,
    len_send,
    len_recv,
    ret_send,
    ret_recv,
    gp_send,
    gp_recv,
):
    rows = q_ref.shape[0]
    dim = win.shape[1] // 2
    heads = q_ref.shape[1] // dim
    tiles = rows // TILE
    block = pkv_hbm.shape[1]
    prefix = pfx.shape[0]
    span = rows + TILE
    responses = lens_ref.shape[1]
    scale = dim ** (-0.5)
    my_p = lax.axis_index("prompt")
    me = lax.axis_index("seq")
    has_next = me < n_seq - 1
    has_prev = me > 0

    seq_peers = [lax.rem(me + d, n_seq) for d in range(1, n_seq)]
    prompt_peers = [lax.rem(my_p + d, n_prompt) for d in range(1, n_prompt)]

    barrier = pltpu.get_barrier_semaphore()
    for peer in seq_peers:
        pl.semaphore_signal(
            barrier, inc=1, device_id=(my_p, peer), device_id_type=pl.DeviceIdType.MESH
        )
    for peer in prompt_peers:
        pl.semaphore_signal(
            barrier, inc=1, device_id=(peer, me), device_id_type=pl.DeviceIdType.MESH
        )

    own_block = pl.ds(pl.multiple_of(me * block, 16), block)
    loads = [
        pltpu.make_async_copy(kv_hbm.at[0], win.at[pl.ds(rows, rows)], in_sem.at[0]),
        pltpu.make_async_copy(pkv_hbm.at[0], pfx.at[own_block], in_sem.at[1]),
        pltpu.make_async_copy(q_hbm.at[0], q_ref, in_sem.at[2]),
        pltpu.make_async_copy(up_hbm.at[0], up_ref, in_sem.at[3]),
    ]
    for load in loads:
        load.start()

    total = lens_ref[0, 0]
    for r in range(1, responses):
        total = total + lens_ref[0, r]
    lens_all[my_p] = jnp.full((8, 128), total, jnp.int32).astype(F32)

    pl.semaphore_wait(barrier, n_seq - 1 + n_prompt - 1)

    def remote(src, dst, send, recv, target):
        return pltpu.make_async_remote_copy(
            src_ref=src,
            dst_ref=dst,
            send_sem=send,
            recv_sem=recv,
            device_id=target,
            device_id_type=pl.DeviceIdType.MESH,
        )

    def part(j):
        return pl.ds(j * TILE, TILE)

    def prev_copy(j):
        return remote(
            kv_hbm.at[0, part(j)],
            win.at[part(j)],
            prev_send.at[j],
            prev_recv.at[j],
            (my_p, me + 1),
        )

    def ret_copy(j):
        return remote(
            ret_out.at[part(j)],
            ret_in.at[part(j)],
            ret_send.at[j],
            ret_recv.at[j],
            (my_p, me - 1),
        )

    def pf_copy(d, sender, target):
        rows_of = pl.ds(pl.multiple_of(sender * block, 16), block)
        return remote(
            pkv_hbm.at[0], pfx.at[rows_of], pf_send.at[d], pf_recv.at[sender], (my_p, target)
        )

    def len_copy(d, sender, target):
        return remote(
            lens_all.at[sender],
            lens_all.at[sender],
            len_send.at[d],
            len_recv.at[sender],
            (target, me),
        )

    def gp_copy(d, sender, target):
        rows_of = pl.ds(pl.multiple_of(target * block, 16), block)
        return remote(
            gp_out.at[rows_of],
            gp_in.at[sender],
            gp_send.at[d],
            gp_recv.at[sender],
            (my_p, target),
        )

    order = [tiles - 1] + list(range(tiles - 1))
    for d, peer in enumerate(seq_peers):
        pf_copy(d, me, peer).start()

    @pl.when(has_next)
    def _():
        prev_copy(order[0]).start()

    for d, peer in enumerate(prompt_peers):
        len_copy(d, my_p, peer).start()

    @pl.when(has_next)
    def _():
        for j in order[1:]:
            prev_copy(j).start()

    @pl.when(jnp.logical_not(has_prev))
    def _():
        win[pl.ds(0, rows)] = jnp.zeros((rows, 2 * dim), BF16)

    @pl.when(jnp.logical_not(has_next))
    def _():
        ret_in[...] = jnp.zeros((rows, 2 * dim), BF16)

    acc[...] = jnp.zeros_like(acc)
    acc_p[...] = jnp.zeros_like(acc_p)
    win_vt[pl.ds(dim, ONES)] = jnp.ones((ONES, 2 * rows), BF16)
    pfx_vt[pl.ds(dim, ONES)] = jnp.ones((ONES, pfx.shape[0]), BF16)

    def turn(j):
        keys = win[part(j), :dim]
        values = win[part(j), dim:]
        win_kt[:, part(j)] = keys.T
        win_vt[pl.ds(0, dim), part(j)] = values.T

    loads[0].wait()
    for j in range(tiles, 2 * tiles):
        turn(j)
    for load in loads[1:]:
        load.wait()
    for d, peer in enumerate(seq_peers):
        pf_copy(d, peer, me).wait_recv()
    pfx_kt[...] = pfx[:, :dim].T
    pfx_vt[pl.ds(0, dim)] = pfx[:, dim:].T

    @pl.when(has_prev)
    def _():
        prev_copy(order[0]).wait_recv()

    turn(order[0])
    for d, peer in enumerate(prompt_peers):
        len_copy(d, peer, my_p).wait_recv()
    tokens = lens_all[0]
    for p in range(1, n_prompt):
        tokens = tokens + lens_all[p]
    factor = (F32(n_prompt * n_seq * rows) / tokens)[:1]
    factor2 = jnp.concatenate([factor] * PAIR, axis=1)

    def out_copies(i):
        return (
            pltpu.make_async_copy(
                att.at[part(i)], att_hbm.at[0, part(i)], out_sem.at[2 * i]
            ),
            pltpu.make_async_copy(
                gq.at[part(i)], gq_hbm.at[0, part(i)], out_sem.at[2 * i + 1]
            ),
        )

    def tile_step(i):
        start_row = pl.multiple_of(i * TILE, TILE)
        own = pl.ds(start_row, TILE)
        window = pl.ds(start_row, span)

        slots = me * rows + start_row + lax.broadcasted_iota(jnp.int32, (1, TILE), 1)
        first = jnp.zeros((1, TILE), jnp.int32)
        end = jnp.int32(0)
        for r in range(responses):
            end = end + lens_ref[0, r]
            first = jnp.where(slots >= end, end, first)
        live = jnp.where(slots < end, F32(1), F32(0))
        live2 = jnp.concatenate([live] * PAIR, axis=1)
        key_slots = (me - 1) * rows + start_row + lax.broadcasted_iota(jnp.int32, (span, TILE), 0)
        seen = (key_slots >= first) & (key_slots <= slots)
        bias[...] = jnp.where(seen, F32(0), F32(HIDDEN))

        q_of, top_of, g_of, delta_of = {}, {}, {}, {}
        pairs = heads // PAIR
        width = PAIR * TILE
        chunks = [(pfx, pl.ds(lo, min(TILE, prefix - lo)), pl.ds(lo, min(TILE, prefix - lo)), None)
                  for lo in range(0, prefix, TILE)]
        chunks += [
            (
                win,
                pl.ds(pl.multiple_of(start_row + lo, TILE), TILE),
                pl.ds(prefix + lo, TILE),
                pl.ds(lo, TILE),
            )
            for lo in range(0, span, TILE)
        ]

        def cols_of(pair):
            return [pl.ds((pair * PAIR + k) * dim, dim) for k in range(PAIR)]

        def score_stage(pair):
            def begin():
                q_of[pair] = jnp.concatenate([q_ref[own, c] for c in cols_of(pair)], axis=0)
                top_of[pair] = []

            def chunk(source, keys, at, mask_rows):
                s = mm_nt(source[keys, :dim], q_of[pair])
                if mask_rows is not None:
                    hide = bias[mask_rows]
                    s = s + jnp.concatenate([hide] * PAIR, axis=1)
                s_ref[pair % 2, at] = s
                top_of[pair].append(jnp.max(s.reshape(-1, 8, width), axis=0))

            def end():
                top_of[pair] = jnp.max(
                    functools.reduce(jnp.maximum, top_of[pair]), axis=0, keepdims=True
                )

            return begin, chunk, end

        def weight_stage(pair):
            step = scale * math.log2(math.e)
            lanes = pl.ds(pair * width, width)

            def begin():
                pass

            def chunk(source, keys, at, mask_rows):
                w_ref[at, lanes] = jnp.exp2((s_ref[pair % 2, at] - top_of[pair]) * step).astype(
                    BF16
                )

            def end():
                mixed = mm(pfx_vt[...], w_ref[pl.ds(0, prefix), lanes])
                mixed = mixed + mm(win_vt[:, window], w_ref[pl.ds(prefix, span), lanes])
                inverse = live2 / mixed[dim : dim + 1]
                att_t = (mixed[:dim] * inverse).astype(BF16)
                up_t = jnp.concatenate([up_ref[own, c].T for c in cols_of(pair)], axis=1)
                g_t = (up_t.astype(F32) * inverse).astype(BF16)
                g_of[pair] = g_t
                delta_of[pair] = jnp.sum(
                    g_t.astype(F32) * att_t.astype(F32), axis=0, keepdims=True
                )
                for k, c in enumerate(cols_of(pair)):
                    att[own, c] = att_t[:, k * TILE : (k + 1) * TILE].T

            return begin, chunk, end

        def grad_stage(pair):
            lanes = pl.ds(pair * width, width)

            def begin():
                pass

            def chunk(source, keys, at, mask_rows):
                dp = mm(source[keys, dim:], g_of[pair]) - delta_of[pair]
                d_ref[at, lanes] = (w_ref[at, lanes].astype(F32) * dp).astype(BF16)

            def end():
                gq_t = mm(pfx_kt[...], d_ref[pl.ds(0, prefix), lanes])
                gq_t = gq_t + mm(win_kt[:, window], d_ref[pl.ds(prefix, span), lanes])
                gq_t = (gq_t * (factor2 * scale)).astype(BF16)
                for k, c in enumerate(cols_of(pair)):
                    gq[own, c] = gq_t[:, k * TILE : (k + 1) * TILE].T
                if pair % 2 == 1:
                    both = pl.ds((pair - 1) * width, 2 * width)
                    q_all = jnp.concatenate([q_of[pair - 1], q_of[pair]], axis=0)
                    g_all = jnp.concatenate([g_of[pair - 1], g_of[pair]], axis=1)
                    top_rows, low_rows = pl.ds(0, prefix), pl.ds(prefix, span)
                    acc_p[:, :dim] += mm(d_ref[top_rows, both], q_all)
                    acc[window, :dim] += mm(d_ref[low_rows, both], q_all)
                    acc_p[:, dim:] += mm_nt(w_ref[top_rows, both], g_all)
                    acc[window, dim:] += mm_nt(w_ref[low_rows, both], g_all)

            return begin, chunk, end

        for t in range(pairs + 2):
            running = []
            if t < pairs:
                running.append(score_stage(t))
            if 0 <= t - 1 < pairs:
                running.append(weight_stage(t - 1))
            if 0 <= t - 2 < pairs:
                running.append(grad_stage(t - 2))
            for begin, _, _ in running:
                begin()
            for each in chunks:
                for _, chunk, _ in running:
                    chunk(*each)
            for _, _, end in running:
                end()

    def give_back(j):
        ret_out[part(j)] = acc[part(j)].astype(BF16)

        @pl.when(has_prev)
        def _():
            ret_copy(j).start()

    def round_step(s, carry):
        i = lax.rem(s + tiles - 1, tiles)

        @pl.when(s == 1)
        def _():
            @pl.when(has_prev)
            def _():
                for j in order[1:]:
                    prev_copy(j).wait_recv()

            for j in order[1:]:
                turn(j)

        tile_step(i)
        for copy in out_copies(i):
            copy.start()
        for k in range(1, tiles - 1):

            @pl.when(s == k)
            def _():
                give_back(k - 1)

        return carry

    lax.fori_loop(0, tiles, round_step, 0)

    gp_out[...] = acc_p[...].astype(BF16)
    for d, peer in enumerate(seq_peers):
        gp_copy(d, me, peer).start()
    for j in (tiles - 2, tiles - 1):
        give_back(j)

    final = jnp.concatenate([factor * scale, factor], axis=1)
    for j in range(tiles):

        @pl.when(has_next)
        def _():
            pltpu.make_async_remote_copy(
                src_ref=ret_out.at[part(j)],
                dst_ref=ret_in.at[part(j)],
                send_sem=ret_send.at[j],
                recv_sem=ret_recv.at[j],
                device_id=(my_p, me + 1),
                device_id_type=pl.DeviceIdType.MESH,
            ).wait_recv()

        gkv[part(j)] = (acc[part(tiles + j)] + ret_in[part(j)].astype(F32)) * final
    gkv_copy = pltpu.make_async_copy(gkv, gkv_hbm.at[0], out_sem.at[2 * tiles])
    gkv_copy.start()

    sums = acc_p[own_block]
    for d, peer in enumerate(seq_peers):
        gp_copy(d, peer, me).wait_recv()
        sums = sums + gp_in[peer].astype(F32)
    gpf[...] = sums * final
    gpf_copy = pltpu.make_async_copy(gpf, gpf_hbm.at[0], out_sem.at[2 * tiles + 1])
    gpf_copy.start()

    for d, peer in enumerate(seq_peers):
        pf_copy(d, me, peer).wait_send()
        gp_copy(d, me, peer).wait_send()
    for d, peer in enumerate(prompt_peers):
        len_copy(d, my_p, peer).wait_send()

    @pl.when(has_next)
    def _():
        for j in order:
            prev_copy(j).wait_send()

    @pl.when(has_prev)
    def _():
        for j in range(tiles):
            ret_copy(j).wait_send()

    for i in range(tiles):
        for copy in out_copies(i):
            copy.wait()
    gkv_copy.wait()
    gpf_copy.wait()


def hand_over(*refs):
    half = (len(refs) - 1) // 2
    sources, targets, sems = refs[:half], refs[half : 2 * half], refs[-1]
    copies = []
    for a, (source, target) in enumerate(zip(sources, targets)):
        pieces = 4 if source.shape[1] % 64 == 0 else 1
        step = source.shape[1] // pieces
        for p in range(pieces):
            rows = pl.ds(p * step, step)
            copies.append(
                pltpu.make_async_copy(source.at[0, rows], target.at[0, rows], sems.at[a, p])
            )
    for copy in copies:
        copy.start()
    for copy in copies:
        copy.wait()


def body(n_prompt, n_seq, queries, resp_kv, prefix_kv, lengths, upstream):
    rows, width = queries.shape[1:]
    dim = resp_kv.shape[2] // 2
    block = prefix_kv.shape[1]
    prefix = block * n_seq
    tiles = rows // TILE
    dma = pltpu.SemaphoreType.DMA
    anywhere = pl.BlockSpec(memory_space=pl.ANY)
    vmem = pltpu.VMEM
    out_shape = (
        jax.ShapeDtypeStruct(queries.shape, BF16),
        jax.ShapeDtypeStruct(queries.shape, BF16),
        jax.ShapeDtypeStruct(resp_kv.shape, F32),
        jax.ShapeDtypeStruct(prefix_kv.shape, F32),
    )
    results = pl.pallas_call(
        functools.partial(kernel, n_prompt, n_seq),
        out_shape=out_shape,
        in_specs=[pl.BlockSpec(memory_space=pltpu.SMEM)] + [anywhere] * 4,
        out_specs=(anywhere,) * 4,
        scratch_shapes=[
            vmem((rows, width), BF16),
            vmem((rows, width), BF16),
            vmem((2 * rows, 2 * dim), BF16),
            vmem((prefix, 2 * dim), BF16),
            vmem((dim, 2 * rows), BF16),
            vmem((dim + ONES, 2 * rows), BF16),
            vmem((dim, prefix), BF16),
            vmem((dim + ONES, prefix), BF16),
            vmem((rows + TILE, TILE), F32),
            vmem((2, prefix + rows + TILE, PAIR * TILE), F32),
            vmem((prefix + rows + TILE, width), BF16),
            vmem((prefix + rows + TILE, width), BF16),
            vmem((rows, width), BF16),
            vmem((rows, width), BF16),
            vmem((2 * rows, 2 * dim), F32),
            vmem((prefix, 2 * dim), F32),
            vmem((rows, 2 * dim), BF16),
            vmem((rows, 2 * dim), BF16),
            vmem((prefix, 2 * dim), BF16),
            vmem((n_seq, block, 2 * dim), BF16),
            vmem((rows, 2 * dim), F32),
            vmem((block, 2 * dim), F32),
            vmem((n_prompt, 8, 128), F32),
            dma((4,)),
            dma((2 * tiles + 2,)),
            dma((n_seq,)),
            dma((n_seq,)),
            dma((tiles,)),
            dma((tiles,)),
            dma((n_prompt,)),
            dma((n_prompt,)),
            dma((tiles,)),
            dma((tiles,)),
            dma((n_seq,)),
            dma((n_seq,)),
        ],
        compiler_params=pltpu.CompilerParams(
            collective_id=0, has_side_effects=True, vmem_limit_bytes=62 * 1024 * 1024
        ),
        name="attention_core",
    )(lengths, queries, resp_kv, prefix_kv, upstream)
    return pl.pallas_call(
        hand_over,
        out_shape=out_shape,
        in_specs=[anywhere] * 4,
        out_specs=(anywhere,) * 4,
        scratch_shapes=[dma((4, 4))],
        name="hand_over",
    )(*results)


def solution(mesh):
    spec = P("prompt", "seq", None)
    return jax.shard_map(
        functools.partial(body, mesh.shape["prompt"], mesh.shape["seq"]),
        mesh=mesh,
        in_specs=(spec, spec, spec, P("prompt", None), spec),
        out_specs=(spec, spec, spec, spec),
        check_vma=False,
    )
```

```python
import functools
import math

import jax
import jax.numpy as jnp
from jax import lax
from jax.experimental import pallas as pl
from jax.experimental.pallas import tpu as pltpu
from jax.sharding import PartitionSpec as P

F32 = jnp.float32
BF16 = jnp.bfloat16
TILE = 128
HIDDEN = -1e30
PAIR = 2
ONES = 16


def mm(a, b):
    return lax.dot_general(a, b, (((1,), (0,)), ((), ())), preferred_element_type=F32)


def mm_nt(a, b):
    return lax.dot_general(a, b, (((1,), (1,)), ((), ())), preferred_element_type=F32)


def kernel(
    n_prompt,
    n_seq,
    lens_ref,
    q_hbm,
    kv_hbm,
    pkv_hbm,
    up_hbm,
    att_hbm,
    gq_hbm,
    gkv_hbm,
    gpf_hbm,
    q_ref,
    up_ref,
    win,
    pfx,
    win_kt,
    win_vt,
    pfx_kt,
    pfx_vt,
    bias,
    s_ref,
    top_ref,
    w_ref,
    g_ref,
    delta_ref,
    d_ref,
    att,
    gq,
    acc,
    acc_p,
    ret_out,
    ret_in,
    gp_out,
    gp_in,
    gkv,
    gpf,
    lens_all,
    in_sem,
    out_sem,
    last_sem,
    pf_send,
    pf_recv,
    prev_send,
    prev_recv,
    len_send,
    len_recv,
    ret_send,
    ret_recv,
    gp_send,
    gp_recv,
):
    pairs, rows, width = q_ref.shape
    dim = win.shape[1] // 2
    tiles = rows // TILE
    block = pkv_hbm.shape[1]
    prefix = pfx.shape[0]
    span = rows + TILE
    responses = lens_ref.shape[1]
    scale = dim ** (-0.5)
    my_p = lax.axis_index("prompt")
    me = lax.axis_index("seq")
    has_next = me < n_seq - 1
    has_prev = me > 0

    seq_peers = [lax.rem(me + d, n_seq) for d in range(1, n_seq)]
    prompt_peers = [lax.rem(my_p + d, n_prompt) for d in range(1, n_prompt)]

    barrier = pltpu.get_barrier_semaphore()
    for peer in seq_peers:
        pl.semaphore_signal(
            barrier, inc=1, device_id=(my_p, peer), device_id_type=pl.DeviceIdType.MESH
        )
    for peer in prompt_peers:
        pl.semaphore_signal(
            barrier, inc=1, device_id=(peer, me), device_id_type=pl.DeviceIdType.MESH
        )

    own_block = pl.ds(pl.multiple_of(me * block, 16), block)
    loads = [
        pltpu.make_async_copy(kv_hbm.at[0], win.at[pl.ds(rows, rows)], in_sem.at[0]),
        pltpu.make_async_copy(pkv_hbm.at[0], pfx.at[own_block], in_sem.at[1]),
    ]
    for pair in range(pairs):
        lanes = pl.ds(pair * width, width)
        for k, (source, target) in enumerate(((q_hbm, q_ref), (up_hbm, up_ref))):
            loads.append(
                pltpu.make_async_copy(
                    source.at[0, :, lanes], target.at[pair], in_sem.at[2 + 2 * pair + k]
                )
            )
    for load in loads:
        load.start()

    s_ref[1] = jnp.zeros(s_ref.shape[1:], F32)
    top_ref[1] = jnp.zeros(top_ref.shape[1:], F32)
    for slot in (1, 2):
        w_ref[slot] = jnp.zeros(w_ref.shape[1:], BF16)
        g_ref[slot] = jnp.zeros(g_ref.shape[1:], BF16)
    delta_ref[0] = jnp.zeros(delta_ref.shape[1:], F32)
    d_ref[1] = jnp.zeros(d_ref.shape[1:], BF16)

    total = lens_ref[0, 0]
    for r in range(1, responses):
        total = total + lens_ref[0, r]
    lens_all[my_p] = jnp.full((8, 128), total, jnp.int32).astype(F32)

    pl.semaphore_wait(barrier, n_seq - 1 + n_prompt - 1)

    def remote(src, dst, send, recv, target):
        return pltpu.make_async_remote_copy(
            src_ref=src,
            dst_ref=dst,
            send_sem=send,
            recv_sem=recv,
            device_id=target,
            device_id_type=pl.DeviceIdType.MESH,
        )

    def part(j):
        return pl.ds(j * TILE, TILE)

    def prev_copy(j):
        return remote(
            kv_hbm.at[0, part(j)],
            win.at[part(j)],
            prev_send.at[j],
            prev_recv.at[j],
            (my_p, me + 1),
        )

    def ret_copy(j):
        return remote(
            ret_out.at[part(j)],
            ret_in.at[part(j)],
            ret_send.at[j],
            ret_recv.at[j],
            (my_p, me - 1),
        )

    def pf_copy(d, sender, target):
        rows_of = pl.ds(pl.multiple_of(sender * block, 16), block)
        return remote(
            pkv_hbm.at[0], pfx.at[rows_of], pf_send.at[d], pf_recv.at[sender], (my_p, target)
        )

    def len_copy(d, sender, target):
        return remote(
            lens_all.at[sender],
            lens_all.at[sender],
            len_send.at[d],
            len_recv.at[sender],
            (target, me),
        )

    def gp_copy(d, sender, target):
        rows_of = pl.ds(pl.multiple_of(target * block, 16), block)
        return remote(
            gp_out.at[rows_of],
            gp_in.at[sender],
            gp_send.at[d],
            gp_recv.at[sender],
            (my_p, target),
        )

    order = [tiles - 1] + list(range(tiles - 1))
    for d, peer in enumerate(seq_peers):
        pf_copy(d, me, peer).start()

    @pl.when(has_next)
    def _():
        prev_copy(order[0]).start()

    for d, peer in enumerate(prompt_peers):
        len_copy(d, my_p, peer).start()

    @pl.when(has_next)
    def _():
        for j in order[1:]:
            prev_copy(j).start()

    @pl.when(jnp.logical_not(has_prev))
    def _():
        win[pl.ds(0, rows)] = jnp.zeros((rows, 2 * dim), BF16)

    @pl.when(jnp.logical_not(has_next))
    def _():
        ret_in[...] = jnp.zeros((rows, 2 * dim), BF16)

    acc[...] = jnp.zeros_like(acc)
    acc_p[...] = jnp.zeros_like(acc_p)
    win_vt[pl.ds(dim, ONES)] = jnp.ones((ONES, 2 * rows), BF16)
    pfx_vt[pl.ds(dim, ONES)] = jnp.ones((ONES, pfx.shape[0]), BF16)

    def turn(j):
        keys = win[part(j), :dim]
        values = win[part(j), dim:]
        win_kt[:, part(j)] = keys.T
        win_vt[pl.ds(0, dim), part(j)] = values.T

    loads[0].wait()
    for j in range(tiles, 2 * tiles):
        turn(j)
    for load in loads[1:]:
        load.wait()
    for d, peer in enumerate(seq_peers):
        pf_copy(d, peer, me).wait_recv()
    pfx_kt[...] = pfx[:, :dim].T
    pfx_vt[pl.ds(0, dim)] = pfx[:, dim:].T

    @pl.when(has_prev)
    def _():
        prev_copy(order[0]).wait_recv()

    turn(order[0])
    for d, peer in enumerate(prompt_peers):
        len_copy(d, peer, my_p).wait_recv()
    tokens = lens_all[0]
    for p in range(1, n_prompt):
        tokens = tokens + lens_all[p]
    factor = (F32(n_prompt * n_seq * rows) / tokens)[:1]
    factor2 = jnp.concatenate([factor] * PAIR, axis=1)

    ends = []
    for r in range(responses):
        ends.append(lens_ref[0, r] + (ends[-1] if ends else 0))
    units = tiles * pairs
    step_scale = scale * math.log2(math.e)

    def out_copies(i):
        copies = []
        for pair in range(pairs):
            lanes = pl.ds(pair * width, width)
            for which, (source, target) in enumerate(((att, att_hbm), (gq, gq_hbm))):
                copies.append(
                    pltpu.make_async_copy(
                        source.at[pair, tile_rows(i)],
                        target.at[0, tile_rows(i), lanes],
                        out_sem.at[i, pair, which],
                    )
                )
        return copies

    def tile_rows(i):
        return pl.ds(pl.multiple_of(i * TILE, TILE), TILE)

    def place(unit):
        unit = jnp.clip(unit, 0, units - 1)
        i = lax.rem(lax.div(unit, pairs) + tiles - 1, tiles)
        return i, lax.rem(unit, pairs)

    def slots_of(i):
        return me * rows + i * TILE + lax.broadcasted_iota(jnp.int32, (1, TILE), 1)

    def set_bias(i):
        slots = slots_of(i)
        first = jnp.zeros((1, TILE), jnp.int32)
        for end in ends:
            first = jnp.where(slots >= end, end, first)
        key_slots = (me - 1) * rows + i * TILE + lax.broadcasted_iota(jnp.int32, (span, TILE), 0)
        seen = (key_slots >= first) & (key_slots <= slots)
        bias[...] = jnp.where(seen, F32(0), F32(HIDDEN))

    def heads_of(ref, pair, i):
        return [ref[pair, tile_rows(i), k * dim : (k + 1) * dim] for k in range(PAIR)]

    def put_heads(ref, pair, i, value_t):
        for k in range(PAIR):
            ref[pair, tile_rows(i), k * dim : (k + 1) * dim] = value_t[
                :, k * TILE : (k + 1) * TILE
            ].T

    def pipeline_step(u):
        a_tile, a_pair = place(u)
        b_tile, b_pair = place(u - 1)
        c_tile, _ = place(u - 2)
        d_tile, d_pair = place(u - 3)
        two = lambda v: lax.rem(v + 4, 2)
        four = lambda v: lax.rem(v + 4, 4)
        a_s, b_s = two(u), two(u - 1)
        b_w, c_w, d_w = four(u - 1), four(u - 2), four(u - 3)
        c_d, d_d = two(u - 2), two(u - 3)
        low_rows, top_rows = pl.ds(prefix, span), pl.ds(0, prefix)

        def window(i, lo=0, size=span):
            return pl.ds(pl.multiple_of(i * TILE + lo, TILE), size)

        q_a = jnp.concatenate(heads_of(q_ref, a_pair, a_tile), axis=0)
        b_top = jnp.max(top_ref[b_s], axis=0, keepdims=True)
        g_c = g_ref[c_w]
        delta_c = delta_ref[two(u - 2), 0:1]
        q_d = jnp.concatenate(heads_of(q_ref, d_pair, d_tile), axis=0)
        g_d = g_ref[d_w]

        tops = []
        chunks = [(True, lo, min(TILE, prefix - lo)) for lo in range(0, prefix, TILE)]
        chunks += [(False, lo, TILE) for lo in range(0, span, TILE)]

        def piece(in_prefix, lo, size, i):
            if in_prefix:
                return pfx[pl.ds(lo, size)]
            return win[window(i, lo, size)]

        def chunk(in_prefix, lo, size):
            at = pl.ds(lo if in_prefix else prefix + lo, size)
            score = mm_nt(piece(in_prefix, lo, size, a_tile)[:, :dim], q_a)
            if not in_prefix:
                score = score + jnp.concatenate([bias[pl.ds(lo, size)]] * PAIR, axis=1)
            s_ref[a_s, at] = score
            tops.append(jnp.max(score.reshape(-1, 8, width), axis=0))
            w_ref[b_w, at] = jnp.exp2((s_ref[b_s, at] - b_top) * step_scale).astype(BF16)
            dp = mm(piece(in_prefix, lo, size, c_tile)[:, dim:], g_c) - delta_c
            d_ref[c_d, at] = (w_ref[c_w, at].astype(F32) * dp).astype(BF16)

        half = len(chunks) // 2
        acc_p[:, :dim] += mm(d_ref[d_d, top_rows], q_d)
        acc_p[:, dim:] += mm_nt(w_ref[d_w, top_rows], g_d)
        for each in chunks[:half]:
            chunk(*each)
        acc[window(d_tile), :dim] += mm(d_ref[d_d, low_rows], q_d)
        for each in chunks[half:]:
            chunk(*each)
        top_ref[a_s] = functools.reduce(jnp.maximum, tops)
        mixed = mm(pfx_vt[...], w_ref[b_w, top_rows])
        mixed = mixed + mm(win_vt[:, window(b_tile)], w_ref[b_w, low_rows])
        acc[window(d_tile), dim:] += mm_nt(w_ref[d_w, low_rows], g_d)
        gq_t = mm(pfx_kt[...], d_ref[d_d, top_rows])
        gq_t = gq_t + mm(win_kt[:, window(d_tile)], d_ref[d_d, low_rows])
        put_heads(gq, d_pair, d_tile, (gq_t * (factor2 * scale)).astype(BF16))

        counted = jnp.where((slots_of(b_tile) < ends[-1]) & (u >= 1), F32(1), F32(0))
        inverse = jnp.concatenate([counted] * PAIR, axis=1) / mixed[dim : dim + 1]
        att_t = (mixed[:dim] * inverse).astype(BF16)
        up_t = jnp.concatenate([v.T for v in heads_of(up_ref, b_pair, b_tile)], axis=1)
        g_t = (up_t.astype(F32) * inverse).astype(BF16)
        g_ref[b_w] = g_t
        delta_ref[b_s, 0:1] = jnp.sum(g_t.astype(F32) * att_t.astype(F32), axis=0, keepdims=True)
        put_heads(att, b_pair, b_tile, att_t)

    def give_back(j):
        ret_out[part(j)] = acc[part(j)].astype(BF16)

        @pl.when(has_prev)
        def _():
            ret_copy(j).start()

    def loop_step(u, carry):
        @pl.when((lax.rem(u, pairs) == 0) & (u < units))
        def _():
            set_bias(place(u)[0])

        @pl.when(u == pairs)
        def _():
            @pl.when(has_prev)
            def _():
                for j in order[1:]:
                    prev_copy(j).wait_recv()

            for j in order[1:]:
                turn(j)

        for k in range(tiles - 1):

            @pl.when(u == (k + 1) * pairs + 3)
            def _():
                for copy in out_copies(order[k]):
                    copy.start()
                if k >= 1:
                    give_back(k - 1)

        pipeline_step(u)
        return carry

    lax.fori_loop(0, units + 3, loop_step, 0)

    for copy in out_copies(order[-1]):
        copy.start()
    gp_out[...] = acc_p[...].astype(BF16)
    for d, peer in enumerate(seq_peers):
        gp_copy(d, me, peer).start()
    for j in (tiles - 2, tiles - 1):
        give_back(j)

    final = jnp.concatenate([factor * scale, factor], axis=1)
    for j in range(tiles):

        @pl.when(has_next)
        def _():
            pltpu.make_async_remote_copy(
                src_ref=ret_out.at[part(j)],
                dst_ref=ret_in.at[part(j)],
                send_sem=ret_send.at[j],
                recv_sem=ret_recv.at[j],
                device_id=(my_p, me + 1),
                device_id_type=pl.DeviceIdType.MESH,
            ).wait_recv()

        gkv[part(j)] = (acc[part(tiles + j)] + ret_in[part(j)].astype(F32)) * final
    gkv_copy = pltpu.make_async_copy(gkv, gkv_hbm.at[0], last_sem.at[0])
    gkv_copy.start()

    sums = acc_p[own_block]
    for d, peer in enumerate(seq_peers):
        gp_copy(d, peer, me).wait_recv()
        sums = sums + gp_in[peer].astype(F32)
    gpf[...] = sums * final
    gpf_copy = pltpu.make_async_copy(gpf, gpf_hbm.at[0], last_sem.at[1])
    gpf_copy.start()

    for d, peer in enumerate(seq_peers):
        pf_copy(d, me, peer).wait_send()
        gp_copy(d, me, peer).wait_send()
    for d, peer in enumerate(prompt_peers):
        len_copy(d, my_p, peer).wait_send()

    @pl.when(has_next)
    def _():
        for j in order:
            prev_copy(j).wait_send()

    @pl.when(has_prev)
    def _():
        for j in range(tiles):
            ret_copy(j).wait_send()

    for i in range(tiles):
        for copy in out_copies(i):
            copy.wait()
    gkv_copy.wait()
    gpf_copy.wait()


def hand_over(*refs):
    half = (len(refs) - 1) // 2
    sources, targets, sems = refs[:half], refs[half : 2 * half], refs[-1]
    copies = []
    for a, (source, target) in enumerate(zip(sources, targets)):
        pieces = 4 if source.shape[1] % 64 == 0 else 1
        step = source.shape[1] // pieces
        for p in range(pieces):
            rows = pl.ds(p * step, step)
            copies.append(
                pltpu.make_async_copy(source.at[0, rows], target.at[0, rows], sems.at[a, p])
            )
    for copy in copies:
        copy.start()
    for copy in copies:
        copy.wait()


def body(n_prompt, n_seq, queries, resp_kv, prefix_kv, lengths, upstream):
    rows, width = queries.shape[1:]
    dim = resp_kv.shape[2] // 2
    block = prefix_kv.shape[1]
    prefix = block * n_seq
    tiles = rows // TILE
    keys = prefix + rows + TILE
    lanes = PAIR * dim
    pairs = width // lanes
    dma = pltpu.SemaphoreType.DMA
    anywhere = pl.BlockSpec(memory_space=pl.ANY)
    vmem = pltpu.VMEM
    out_shape = (
        jax.ShapeDtypeStruct(queries.shape, BF16),
        jax.ShapeDtypeStruct(queries.shape, BF16),
        jax.ShapeDtypeStruct(resp_kv.shape, F32),
        jax.ShapeDtypeStruct(prefix_kv.shape, F32),
    )
    results = pl.pallas_call(
        functools.partial(kernel, n_prompt, n_seq),
        out_shape=out_shape,
        in_specs=[pl.BlockSpec(memory_space=pltpu.SMEM)] + [pl.BlockSpec(memory_space=pltpu.HBM)] * 4,
        out_specs=(anywhere,) * 4,
        scratch_shapes=[
            vmem((pairs, rows, lanes), BF16),
            vmem((pairs, rows, lanes), BF16),
            vmem((2 * rows, 2 * dim), BF16),
            vmem((prefix, 2 * dim), BF16),
            vmem((dim, 2 * rows), BF16),
            vmem((dim + ONES, 2 * rows), BF16),
            vmem((dim, prefix), BF16),
            vmem((dim + ONES, prefix), BF16),
            vmem((rows + TILE, TILE), F32),
            vmem((2, keys, lanes), F32),
            vmem((2, 8, lanes), F32),
            vmem((4, keys, lanes), BF16),
            vmem((4, dim, lanes), BF16),
            vmem((2, 8, lanes), F32),
            vmem((2, keys, lanes), BF16),
            vmem((pairs, rows, lanes), BF16),
            vmem((pairs, rows, lanes), BF16),
            vmem((2 * rows, 2 * dim), F32),
            vmem((prefix, 2 * dim), F32),
            vmem((rows, 2 * dim), BF16),
            vmem((rows, 2 * dim), BF16),
            vmem((prefix, 2 * dim), BF16),
            vmem((n_seq, block, 2 * dim), BF16),
            vmem((rows, 2 * dim), F32),
            vmem((block, 2 * dim), F32),
            vmem((n_prompt, 8, 128), F32),
            dma((2 + 2 * pairs,)),
            dma((tiles, pairs, 2)),
            dma((2,)),
            dma((n_seq,)),
            dma((n_seq,)),
            dma((tiles,)),
            dma((tiles,)),
            dma((n_prompt,)),
            dma((n_prompt,)),
            dma((tiles,)),
            dma((tiles,)),
            dma((n_seq,)),
            dma((n_seq,)),
        ],
        compiler_params=pltpu.CompilerParams(
            collective_id=0, has_side_effects=True, vmem_limit_bytes=50 * 1024 * 1024
        ),
        name="attention_core",
    )(*[pltpu.with_memory_space_constraint(x, pltpu.HBM) for x in (lengths, queries, resp_kv, prefix_kv, upstream)])
    return pl.pallas_call(
        hand_over,
        out_shape=out_shape,
        in_specs=[pl.BlockSpec(memory_space=vmem)] * 4,
        out_specs=(anywhere,) * 4,
        scratch_shapes=[dma((4, 4))],
        name="hand_over",
    )(*results)


def solution(mesh):
    spec = P("prompt", "seq", None)
    return jax.shard_map(
        functools.partial(body, mesh.shape["prompt"], mesh.shape["seq"]),
        mesh=mesh,
        in_specs=(spec, spec, spec, P("prompt", None), spec),
        out_specs=(spec, spec, spec, spec),
        check_vma=False,
    )
```

```python
import functools
import math

import jax
import jax.numpy as jnp
from jax import lax
from jax.experimental import pallas as pl
from jax.experimental.pallas import tpu as pltpu
from jax.sharding import PartitionSpec as P

F32 = jnp.float32
BF16 = jnp.bfloat16
TILE = 128
HIDDEN = -1e30
PAIR = 2
ONES = 16


def mm(a, b):
    return lax.dot_general(a, b, (((1,), (0,)), ((), ())), preferred_element_type=F32)


def mm_nt(a, b):
    return lax.dot_general(a, b, (((1,), (1,)), ((), ())), preferred_element_type=F32)


def kernel(
    n_prompt,
    n_seq,
    lens_ref,
    q_hbm,
    kv_hbm,
    pkv_hbm,
    up_hbm,
    att_hbm,
    gq_hbm,
    gkv_hbm,
    gpf_hbm,
    q_ref,
    up_ref,
    win,
    pfx,
    win_kt,
    win_vt,
    pfx_kt,
    pfx_vt,
    bias,
    s_ref,
    top_ref,
    w_ref,
    g_ref,
    delta_ref,
    d_ref,
    att,
    gq,
    acc,
    acc_p,
    ret_out,
    ret_in,
    gp_out,
    gp_in,
    gkv,
    gpf,
    lens_all,
    in_sem,
    out_sem,
    pf_send,
    pf_recv,
    prev_send,
    prev_recv,
    len_send,
    len_recv,
    ret_send,
    ret_recv,
    gp_send,
    gp_recv,
):
    rows = q_ref.shape[0]
    dim = win.shape[1] // 2
    heads = q_ref.shape[1] // dim
    tiles = rows // TILE
    block = pkv_hbm.shape[1]
    prefix = pfx.shape[0]
    span = rows + TILE
    responses = lens_ref.shape[1]
    scale = dim ** (-0.5)
    my_p = lax.axis_index("prompt")
    me = lax.axis_index("seq")
    has_next = me < n_seq - 1
    has_prev = me > 0

    seq_peers = [lax.rem(me + d, n_seq) for d in range(1, n_seq)]
    prompt_peers = [lax.rem(my_p + d, n_prompt) for d in range(1, n_prompt)]

    barrier = pltpu.get_barrier_semaphore()
    for peer in seq_peers:
        pl.semaphore_signal(
            barrier, inc=1, device_id=(my_p, peer), device_id_type=pl.DeviceIdType.MESH
        )
    for peer in prompt_peers:
        pl.semaphore_signal(
            barrier, inc=1, device_id=(peer, me), device_id_type=pl.DeviceIdType.MESH
        )

    own_block = pl.ds(pl.multiple_of(me * block, 16), block)
    loads = [
        pltpu.make_async_copy(kv_hbm.at[0], win.at[pl.ds(rows, rows)], in_sem.at[0]),
        pltpu.make_async_copy(pkv_hbm.at[0], pfx.at[own_block], in_sem.at[1]),
    ]
    for load in loads:
        load.start()

    def row_loads(i):
        some = pl.ds(pl.multiple_of(i * TILE, TILE), TILE)
        return (
            pltpu.make_async_copy(q_hbm.at[0, some], q_ref.at[some], in_sem.at[2 + 2 * i]),
            pltpu.make_async_copy(up_hbm.at[0, some], up_ref.at[some], in_sem.at[3 + 2 * i]),
        )

    order = [tiles - 1] + list(range(tiles - 1))
    for i in order:
        for load in row_loads(i):
            load.start()

    last = heads // PAIR - 1
    late = pl.ds((last - 1) * PAIR * TILE, 2 * PAIR * TILE)
    s_ref[last % 2] = jnp.zeros(s_ref.shape[1:], F32)
    w_ref[:, late] = jnp.zeros((w_ref.shape[0], 2 * PAIR * TILE), BF16)
    for pair in (last - 1, last):
        top_ref[pair] = jnp.zeros(top_ref.shape[1:], F32)
        g_ref[pair] = jnp.zeros(g_ref.shape[1:], BF16)
        delta_ref[pair] = jnp.zeros(delta_ref.shape[1:], F32)

    total = lens_ref[0, 0]
    for r in range(1, responses):
        total = total + lens_ref[0, r]
    lens_all[my_p] = jnp.full((8, 128), total, jnp.int32).astype(F32)

    pl.semaphore_wait(barrier, n_seq - 1 + n_prompt - 1)

    def remote(src, dst, send, recv, target):
        return pltpu.make_async_remote_copy(
            src_ref=src,
            dst_ref=dst,
            send_sem=send,
            recv_sem=recv,
            device_id=target,
            device_id_type=pl.DeviceIdType.MESH,
        )

    def part(j):
        return pl.ds(j * TILE, TILE)

    def prev_copy(j):
        return remote(
            kv_hbm.at[0, part(j)],
            win.at[part(j)],
            prev_send.at[j],
            prev_recv.at[j],
            (my_p, me + 1),
        )

    def ret_copy(j):
        return remote(
            ret_out.at[part(j)],
            ret_in.at[part(j)],
            ret_send.at[j],
            ret_recv.at[j],
            (my_p, me - 1),
        )

    def pf_copy(d, sender, target):
        rows_of = pl.ds(pl.multiple_of(sender * block, 16), block)
        return remote(
            pkv_hbm.at[0], pfx.at[rows_of], pf_send.at[d], pf_recv.at[sender], (my_p, target)
        )

    def len_copy(d, sender, target):
        return remote(
            lens_all.at[sender],
            lens_all.at[sender],
            len_send.at[d],
            len_recv.at[sender],
            (target, me),
        )

    def gp_copy(d, sender, target):
        rows_of = pl.ds(pl.multiple_of(target * block, 16), block)
        return remote(
            gp_out.at[rows_of],
            gp_in.at[sender],
            gp_send.at[d],
            gp_recv.at[sender],
            (my_p, target),
        )

    for d, peer in enumerate(seq_peers):
        pf_copy(d, me, peer).start()

    @pl.when(has_next)
    def _():
        prev_copy(order[0]).start()

    for d, peer in enumerate(prompt_peers):
        len_copy(d, my_p, peer).start()

    @pl.when(has_next)
    def _():
        for j in order[1:]:
            prev_copy(j).start()

    @pl.when(jnp.logical_not(has_prev))
    def _():
        win[pl.ds(0, rows)] = jnp.zeros((rows, 2 * dim), BF16)

    @pl.when(jnp.logical_not(has_next))
    def _():
        ret_in[...] = jnp.zeros((rows, 2 * dim), BF16)

    acc[...] = jnp.zeros_like(acc)
    acc_p[...] = jnp.zeros_like(acc_p)
    win_vt[pl.ds(dim, ONES)] = jnp.ones((ONES, 2 * rows), BF16)
    pfx_vt[pl.ds(dim, ONES)] = jnp.ones((ONES, pfx.shape[0]), BF16)

    def turn(j):
        keys = win[part(j), :dim]
        values = win[part(j), dim:]
        win_kt[:, part(j)] = keys.T
        win_vt[pl.ds(0, dim), part(j)] = values.T

    loads[0].wait()
    for j in range(tiles, 2 * tiles):
        turn(j)
    for load in loads[1:]:
        load.wait()
    for d, peer in enumerate(seq_peers):
        pf_copy(d, peer, me).wait_recv()
    pfx_kt[...] = pfx[:, :dim].T
    pfx_vt[pl.ds(0, dim)] = pfx[:, dim:].T

    @pl.when(has_prev)
    def _():
        prev_copy(order[0]).wait_recv()

    turn(order[0])
    for d, peer in enumerate(prompt_peers):
        len_copy(d, peer, my_p).wait_recv()
    tokens = lens_all[0]
    for p in range(1, n_prompt):
        tokens = tokens + lens_all[p]
    factor = (F32(n_prompt * n_seq * rows) / tokens)[:1]
    factor2 = jnp.concatenate([factor] * PAIR, axis=1)

    def out_copies(i):
        return (
            pltpu.make_async_copy(
                att.at[tile_rows(i)], att_hbm.at[0, tile_rows(i)], out_sem.at[2 * i]
            ),
            pltpu.make_async_copy(
                gq.at[tile_rows(i)], gq_hbm.at[0, tile_rows(i)], out_sem.at[2 * i + 1]
            ),
        )

    ends = []
    for r in range(responses):
        ends.append(lens_ref[0, r] + (ends[-1] if ends else 0))
    pairs = heads // PAIR
    width = PAIR * TILE
    step_scale = scale * math.log2(math.e)
    top_rows, low_rows = pl.ds(0, prefix), pl.ds(prefix, span)
    chunks = [(True, lo, min(TILE, prefix - lo)) for lo in range(0, prefix, TILE)]
    chunks += [(False, lo, TILE) for lo in range(0, span, TILE)]

    def tile_rows(i, size=TILE, lo=0):
        return pl.ds(pl.multiple_of(i * TILE + lo, TILE), size)

    def slots_of(i):
        return me * rows + i * TILE + lax.broadcasted_iota(jnp.int32, (1, TILE), 1)

    def set_bias(i):
        slots = slots_of(i)
        first = jnp.zeros((1, TILE), jnp.int32)
        for end in ends:
            first = jnp.where(slots >= end, end, first)
        key_slots = (me - 1) * rows + i * TILE + lax.broadcasted_iota(jnp.int32, (span, TILE), 0)
        seen = (key_slots >= first) & (key_slots <= slots)
        bias[...] = jnp.where(seen, F32(0), F32(HIDDEN))

    def cols_of(pair):
        return [pl.ds((pair * PAIR + k) * dim, dim) for k in range(PAIR)]

    def heads_of(ref, pair, i):
        return [ref[tile_rows(i), c] for c in cols_of(pair)]

    def put_heads(ref, pair, i, value_t):
        for k, c in enumerate(cols_of(pair)):
            ref[tile_rows(i), c] = value_t[:, k * TILE : (k + 1) * TILE].T

    def piece(in_prefix, lo, size, i):
        if in_prefix:
            return pfx[pl.ds(lo, size)]
        return win[tile_rows(i, size, lo)]

    def place_of(in_prefix, lo, size):
        return pl.ds(lo if in_prefix else prefix + lo, size)

    def score_stage(pair, i):
        q_a = jnp.concatenate(heads_of(q_ref, pair, i), axis=0)
        tops = []

        def chunk(in_prefix, lo, size):
            score = mm_nt(piece(in_prefix, lo, size, i)[:, :dim], q_a)
            if not in_prefix:
                score = score + jnp.concatenate([bias[pl.ds(lo, size)]] * PAIR, axis=1)
            s_ref[pair % 2, place_of(in_prefix, lo, size)] = score
            tops.append(jnp.max(score.reshape(-1, 8, width), axis=0))

        def end():
            top_ref[pair] = functools.reduce(jnp.maximum, tops)

        return chunk, end

    def weight_stage(pair, i, counts):
        lanes = pl.ds(pair * width, width)
        top = jnp.max(top_ref[pair], axis=0, keepdims=True)

        def chunk(in_prefix, lo, size):
            at = place_of(in_prefix, lo, size)
            w_ref[at, lanes] = jnp.exp2((s_ref[pair % 2, at] - top) * step_scale).astype(BF16)

        def end():
            mixed = mm(pfx_vt[...], w_ref[top_rows, lanes])
            mixed = mixed + mm(win_vt[:, tile_rows(i, span)], w_ref[low_rows, lanes])
            live = jnp.where((slots_of(i) < ends[-1]) & counts, F32(1), F32(0))
            inverse = jnp.concatenate([live] * PAIR, axis=1) / mixed[dim : dim + 1]
            att_t = (mixed[:dim] * inverse).astype(BF16)
            up_t = jnp.concatenate([v.T for v in heads_of(up_ref, pair, i)], axis=1)
            g_t = (up_t.astype(F32) * inverse).astype(BF16)
            g_ref[pair] = g_t
            delta_ref[pair, 0:1] = jnp.sum(
                g_t.astype(F32) * att_t.astype(F32), axis=0, keepdims=True
            )
            put_heads(att, pair, i, att_t)

        return chunk, end

    def grad_stage(pair, i):
        lanes = pl.ds(pair * width, width)
        g_c = g_ref[pair]
        delta_c = delta_ref[pair, 0:1]

        def chunk(in_prefix, lo, size):
            at = place_of(in_prefix, lo, size)
            dp = mm(piece(in_prefix, lo, size, i)[:, dim:], g_c) - delta_c
            d_ref[at, lanes] = (w_ref[at, lanes].astype(F32) * dp).astype(BF16)

        def end():
            gq_t = mm(pfx_kt[...], d_ref[top_rows, lanes])
            gq_t = gq_t + mm(win_kt[:, tile_rows(i, span)], d_ref[low_rows, lanes])
            put_heads(gq, pair, i, (gq_t * (factor2 * scale)).astype(BF16))
            if pair % 2 == 1:
                both = pl.ds((pair - 1) * width, 2 * width)
                q_all = jnp.concatenate(
                    heads_of(q_ref, pair - 1, i) + heads_of(q_ref, pair, i), axis=0
                )
                g_all = jnp.concatenate([g_ref[pair - 1], g_ref[pair]], axis=1)
                acc_p[:, :dim] += mm(d_ref[top_rows, both], q_all)
                acc[tile_rows(i, span), :dim] += mm(d_ref[low_rows, both], q_all)
                acc_p[:, dim:] += mm_nt(w_ref[top_rows, both], g_all)
                acc[tile_rows(i, span), dim:] += mm_nt(w_ref[low_rows, both], g_all)

        return chunk, end

    def run(stages):
        for each in chunks:
            for chunk, _ in stages:
                chunk(*each)
        for _, end in stages:
            end()

    def give_back(j):
        ret_out[part(j)] = acc[part(j)].astype(BF16)

        @pl.when(has_prev)
        def _():
            ret_copy(j).start()

    def tile_at(k):
        return lax.rem(k + tiles - 1, tiles)

    def round_step(k, carry):
        i, before = tile_at(k), tile_at(jnp.maximum(k - 1, 0))

        @pl.when(k == 1)
        def _():
            @pl.when(has_prev)
            def _():
                for j in order[1:]:
                    prev_copy(j).wait_recv()

            for j in order[1:]:
                turn(j)

        for load in row_loads(i):
            load.wait()

        @pl.when(k >= 2)
        def _():
            for copy in out_copies(tile_at(k - 2)):
                copy.start()

        for r in range(3, tiles):

            @pl.when(k == r)
            def _():
                give_back(r - 3)

        set_bias(i)
        for pair in range(pairs):
            stages = [score_stage(pair, i)]
            if pair >= 1:
                stages.append(weight_stage(pair - 1, i, True))
            else:
                stages.append(weight_stage(pairs - 1, before, k >= 1))
            if pair >= 2:
                stages.append(grad_stage(pair - 2, i))
            else:
                stages.append(grad_stage(pairs - 2 + pair, before))
            run(stages)
        return carry

    lax.fori_loop(0, tiles, round_step, 0)

    for copy in out_copies(order[-2]):
        copy.start()
    for j in range(max(tiles - 3, 0), tiles - 2):
        give_back(j)
    run([weight_stage(pairs - 1, order[-1], True), grad_stage(pairs - 2, order[-1])])
    run([grad_stage(pairs - 1, order[-1])])
    for copy in out_copies(order[-1]):
        copy.start()
    gp_out[...] = acc_p[...].astype(BF16)
    for d, peer in enumerate(seq_peers):
        gp_copy(d, me, peer).start()
    for j in (tiles - 2, tiles - 1):
        give_back(j)

    final = jnp.concatenate([factor * scale, factor], axis=1)
    for j in range(tiles):

        @pl.when(has_next)
        def _():
            pltpu.make_async_remote_copy(
                src_ref=ret_out.at[part(j)],
                dst_ref=ret_in.at[part(j)],
                send_sem=ret_send.at[j],
                recv_sem=ret_recv.at[j],
                device_id=(my_p, me + 1),
                device_id_type=pl.DeviceIdType.MESH,
            ).wait_recv()

        gkv[part(j)] = (acc[part(tiles + j)] + ret_in[part(j)].astype(F32)) * final
    gkv_copy = pltpu.make_async_copy(gkv, gkv_hbm.at[0], out_sem.at[2 * tiles])
    gkv_copy.start()

    sums = acc_p[own_block]
    for d, peer in enumerate(seq_peers):
        gp_copy(d, peer, me).wait_recv()
        sums = sums + gp_in[peer].astype(F32)
    gpf[...] = sums * final
    gpf_copy = pltpu.make_async_copy(gpf, gpf_hbm.at[0], out_sem.at[2 * tiles + 1])
    gpf_copy.start()

    for d, peer in enumerate(seq_peers):
        pf_copy(d, me, peer).wait_send()
        gp_copy(d, me, peer).wait_send()
    for d, peer in enumerate(prompt_peers):
        len_copy(d, my_p, peer).wait_send()

    @pl.when(has_next)
    def _():
        for j in order:
            prev_copy(j).wait_send()

    @pl.when(has_prev)
    def _():
        for j in range(tiles):
            ret_copy(j).wait_send()

    for i in range(tiles):
        for copy in out_copies(i):
            copy.wait()
    gkv_copy.wait()
    gpf_copy.wait()


def body(n_prompt, n_seq, queries, resp_kv, prefix_kv, lengths, upstream):
    rows, width = queries.shape[1:]
    dim = resp_kv.shape[2] // 2
    block = prefix_kv.shape[1]
    prefix = block * n_seq
    tiles = rows // TILE
    pairs = width // (PAIR * dim)
    dma = pltpu.SemaphoreType.DMA
    anywhere = pl.BlockSpec(memory_space=pl.ANY)
    vmem = pltpu.VMEM
    out_shape = (
        jax.ShapeDtypeStruct(queries.shape, BF16),
        jax.ShapeDtypeStruct(queries.shape, BF16),
        jax.ShapeDtypeStruct(resp_kv.shape, F32),
        jax.ShapeDtypeStruct(prefix_kv.shape, F32),
    )
    placed = [
        pltpu.with_memory_space_constraint(x, pltpu.HBM)
        for x in (lengths, queries, resp_kv, prefix_kv, upstream)
    ]
    return pl.pallas_call(
        functools.partial(kernel, n_prompt, n_seq),
        out_shape=out_shape,
        in_specs=[pl.BlockSpec(memory_space=pltpu.SMEM)] + [anywhere] * 4,
        out_specs=(anywhere,) * 4,
        scratch_shapes=[
            vmem((rows, width), BF16),
            vmem((rows, width), BF16),
            vmem((2 * rows, 2 * dim), BF16),
            vmem((prefix, 2 * dim), BF16),
            vmem((dim, 2 * rows), BF16),
            vmem((dim + ONES, 2 * rows), BF16),
            vmem((dim, prefix), BF16),
            vmem((dim + ONES, prefix), BF16),
            vmem((rows + TILE, TILE), F32),
            vmem((2, prefix + rows + TILE, PAIR * TILE), F32),
            vmem((pairs, 8, PAIR * TILE), F32),
            vmem((prefix + rows + TILE, width), BF16),
            vmem((pairs, dim, PAIR * TILE), BF16),
            vmem((pairs, 8, PAIR * TILE), F32),
            vmem((prefix + rows + TILE, width), BF16),
            vmem((rows, width), BF16),
            vmem((rows, width), BF16),
            vmem((2 * rows, 2 * dim), F32),
            vmem((prefix, 2 * dim), F32),
            vmem((rows, 2 * dim), BF16),
            vmem((rows, 2 * dim), BF16),
            vmem((prefix, 2 * dim), BF16),
            vmem((n_seq, block, 2 * dim), BF16),
            vmem((rows, 2 * dim), F32),
            vmem((block, 2 * dim), F32),
            vmem((n_prompt, 8, 128), F32),
            dma((2 + 2 * tiles,)),
            dma((2 * tiles + 2,)),
            dma((n_seq,)),
            dma((n_seq,)),
            dma((tiles,)),
            dma((tiles,)),
            dma((n_prompt,)),
            dma((n_prompt,)),
            dma((tiles,)),
            dma((tiles,)),
            dma((n_seq,)),
            dma((n_seq,)),
        ],
        compiler_params=pltpu.CompilerParams(
            collective_id=0, has_side_effects=True, vmem_limit_bytes=50 * 1024 * 1024
        ),
        name="attention_core",
    )(*placed)


def solution(mesh):
    spec = P("prompt", "seq", None)
    return jax.shard_map(
        functools.partial(body, mesh.shape["prompt"], mesh.shape["seq"]),
        mesh=mesh,
        in_specs=(spec, spec, spec, P("prompt", None), spec),
        out_specs=(spec, spec, spec, spec),
        check_vma=False,
    )
```

```python
import functools
import math

import jax
import jax.numpy as jnp
from jax import lax
from jax.experimental import pallas as pl
from jax.experimental.pallas import tpu as pltpu
from jax.sharding import PartitionSpec as P

F32 = jnp.float32
BF16 = jnp.bfloat16
TILE = 128
HIDDEN = -1e30
PAIR = 2
CHUNK = 128
ONES = 16


def mm(a, b):
    return lax.dot_general(a, b, (((1,), (0,)), ((), ())), preferred_element_type=F32)


def mm_nt(a, b):
    return lax.dot_general(a, b, (((1,), (1,)), ((), ())), preferred_element_type=F32)


def clear(ref, size):
    @pl.loop(0, size // 64)
    def _(j):
        at = pl.ds(pl.multiple_of(j * 64, 64), 64)
        ref[at] = jnp.zeros((64,) + ref.shape[1:], ref.dtype)


def kernel(
    n_prompt,
    n_seq,
    lens_ref,
    q_hbm,
    kv_hbm,
    pkv_hbm,
    up_hbm,
    att_hbm,
    gq_hbm,
    gkv_hbm,
    gpf_hbm,
    q_ref,
    up_ref,
    win,
    pfx,
    win_kt,
    win_vt,
    pfx_kt,
    pfx_vt,
    bias,
    s_ref,
    top_ref,
    w_ref,
    g_ref,
    delta_ref,
    d_ref,
    att,
    gq,
    acc,
    acc_p,
    ret_out,
    ret_in,
    gp_out,
    gp_in,
    gkv,
    gpf,
    lens_all,
    own_sem,
    in_sem,
    out_sem,
    last_sem,
    pf_send,
    pf_recv,
    prev_send,
    prev_recv,
    len_send,
    len_recv,
    ret_send,
    ret_recv,
    gp_send,
    gp_recv,
):
    pairs, rows, width = q_ref.shape
    dim = win.shape[1] // 2
    tiles = rows // TILE
    block = pkv_hbm.shape[1]
    prefix = pfx.shape[0]
    span = rows + TILE
    responses = lens_ref.shape[1]
    scale = dim ** (-0.5)
    my_p = lax.axis_index("prompt")
    me = lax.axis_index("seq")
    has_next = me < n_seq - 1
    has_prev = me > 0

    seq_peers = [lax.rem(me + d, n_seq) for d in range(1, n_seq)]
    prompt_peers = [lax.rem(my_p + d, n_prompt) for d in range(1, n_prompt)]

    barrier = pltpu.get_barrier_semaphore()
    for peer in seq_peers:
        pl.semaphore_signal(
            barrier, inc=1, device_id=(my_p, peer), device_id_type=pl.DeviceIdType.MESH
        )
    for peer in prompt_peers:
        pl.semaphore_signal(
            barrier, inc=1, device_id=(peer, me), device_id_type=pl.DeviceIdType.MESH
        )

    own_block = pl.ds(pl.multiple_of(me * block, 16), block)
    loads = [
        pltpu.make_async_copy(kv_hbm.at[0], win.at[pl.ds(rows, rows)], own_sem.at[0]),
        pltpu.make_async_copy(pkv_hbm.at[0], pfx.at[own_block], own_sem.at[1]),
    ]

    def row_loads(some, group):
        copies = []
        for pair in range(pairs):
            lanes = pl.ds(pair * width, width)
            for k, (source, target) in enumerate(((q_hbm, q_ref), (up_hbm, up_ref))):
                copies.append(
                    pltpu.make_async_copy(
                        source.at[0, some, lanes], target.at[pair, some], in_sem.at[group, pair, k]
                    )
                )
        return copies

    order = [tiles - 1] + list(range(tiles - 1))
    early_rows = row_loads(pl.ds((tiles - 1) * TILE, TILE), 0)
    other_rows = row_loads(pl.ds(0, (tiles - 1) * TILE), 1)
    for load in loads + early_rows + other_rows:
        load.start()

    for ref in (top_ref, g_ref, delta_ref):
        ref[...] = jnp.zeros_like(ref)
    clear(s_ref, s_ref.shape[0])
    clear(w_ref, w_ref.shape[0])

    total = lens_ref[0, 0]
    for r in range(1, responses):
        total = total + lens_ref[0, r]
    lens_all[my_p] = jnp.full((8, 128), total, jnp.int32).astype(F32)

    pl.semaphore_wait(barrier, n_seq - 1 + n_prompt - 1)

    def remote(src, dst, send, recv, target):
        return pltpu.make_async_remote_copy(
            src_ref=src,
            dst_ref=dst,
            send_sem=send,
            recv_sem=recv,
            device_id=target,
            device_id_type=pl.DeviceIdType.MESH,
        )

    def part(j):
        return pl.ds(pl.multiple_of(j * TILE, TILE), TILE)

    def prev_copy(j):
        return remote(
            kv_hbm.at[0, part(j)],
            win.at[part(j)],
            prev_send.at[j],
            prev_recv.at[j],
            (my_p, me + 1),
        )

    def ret_copy(j):
        return remote(
            ret_out.at[part(j)],
            ret_in.at[part(j)],
            ret_send.at[j],
            ret_recv.at[j],
            (my_p, me - 1),
        )

    def pf_copy(d, sender, target):
        rows_of = pl.ds(pl.multiple_of(sender * block, 16), block)
        return remote(
            pkv_hbm.at[0], pfx.at[rows_of], pf_send.at[d], pf_recv.at[sender], (my_p, target)
        )

    def len_copy(d, sender, target):
        return remote(
            lens_all.at[sender],
            lens_all.at[sender],
            len_send.at[d],
            len_recv.at[sender],
            (target, me),
        )

    def gp_copy(d, sender, target):
        rows_of = pl.ds(pl.multiple_of(target * block, 16), block)
        return remote(
            gp_out.at[rows_of],
            gp_in.at[sender],
            gp_send.at[d],
            gp_recv.at[sender],
            (my_p, target),
        )

    for d, peer in enumerate(seq_peers):
        pf_copy(d, me, peer).start()

    @pl.when(has_next)
    def _():
        prev_copy(order[0]).start()

    for d, peer in enumerate(prompt_peers):
        len_copy(d, my_p, peer).start()

    @pl.when(has_next)
    def _():
        for j in order[1:]:
            prev_copy(j).start()

    @pl.when(jnp.logical_not(has_prev))
    def _():
        clear(win, rows)

    @pl.when(jnp.logical_not(has_next))
    def _():
        clear(ret_in, rows)

    clear(acc, 2 * rows)
    clear(acc_p, prefix)
    win_vt[pl.ds(dim, ONES)] = jnp.ones((ONES, 2 * rows), BF16)
    pfx_vt[pl.ds(dim, ONES)] = jnp.ones((ONES, pfx.shape[0]), BF16)

    def turn(j):
        keys = win[part(j), :dim]
        values = win[part(j), dim:]
        win_kt[:, part(j)] = keys.T
        win_vt[pl.ds(0, dim), part(j)] = values.T

    loads[0].wait()
    pl.loop(tiles, 2 * tiles)(turn)
    for load in loads[1:] + early_rows:
        load.wait()
    for d, peer in enumerate(seq_peers):
        pf_copy(d, peer, me).wait_recv()
    pfx_kt[...] = pfx[:, :dim].T
    pfx_vt[pl.ds(0, dim)] = pfx[:, dim:].T

    @pl.when(has_prev)
    def _():
        prev_copy(order[0]).wait_recv()

    turn(order[0])
    for d, peer in enumerate(prompt_peers):
        len_copy(d, peer, my_p).wait_recv()
    tokens = lens_all[0]
    for p in range(1, n_prompt):
        tokens = tokens + lens_all[p]
    factor = (F32(n_prompt * n_seq * rows) / tokens)[:1]
    factor2 = jnp.concatenate([factor] * PAIR, axis=1)

    ends = []
    for r in range(responses):
        ends.append(lens_ref[0, r] + (ends[-1] if ends else 0))
    units = tiles * pairs
    step_scale = scale * math.log2(math.e)

    def out_copies(i):
        copies = []
        for pair in range(pairs):
            lanes = pl.ds(pair * width, width)
            for which, (source, target) in enumerate(((att, att_hbm), (gq, gq_hbm))):
                copies.append(
                    pltpu.make_async_copy(
                        source.at[pair, tile_rows(i)],
                        target.at[0, tile_rows(i), lanes],
                        out_sem.at[i, pair, which],
                    )
                )
        return copies

    def tile_rows(i):
        return pl.ds(pl.multiple_of(i * TILE, TILE), TILE)

    def place(unit):
        unit = jnp.clip(unit, 0, units - 1)
        i = lax.rem(lax.div(unit, pairs) + tiles - 1, tiles)
        return i, lax.rem(unit, pairs)

    def slots_of(i):
        return me * rows + i * TILE + lax.broadcasted_iota(jnp.int32, (1, TILE), 1)

    def set_bias(i):
        slots = slots_of(i)
        first = jnp.zeros((1, TILE), jnp.int32)
        for end in ends:
            first = jnp.where(slots >= end, end, first)
        key_slots = (me - 1) * rows + i * TILE + lax.broadcasted_iota(jnp.int32, (span, TILE), 0)
        seen = (key_slots >= first) & (key_slots <= slots)
        bias[...] = jnp.where(seen, F32(0), F32(HIDDEN))

    def heads_of(ref, pair, i):
        return [ref[pair, tile_rows(i), k * dim : (k + 1) * dim] for k in range(PAIR)]

    def put_heads(ref, pair, i, value_t):
        for k in range(PAIR):
            ref[pair, tile_rows(i), k * dim : (k + 1) * dim] = value_t[
                :, k * TILE : (k + 1) * TILE
            ].T

    def window(i, lo=0, size=span):
        return pl.ds(pl.multiple_of(i * TILE + lo, TILE), size)

    low_rows, top_rows = pl.ds(prefix, span), pl.ds(0, prefix)
    chunks = [(True, lo, min(CHUNK, prefix - lo)) for lo in range(0, prefix, CHUNK)]
    chunks += [(False, lo, min(CHUNK, span - lo)) for lo in range(0, span, CHUNK)]

    def pipeline_step(u):
        a_tile, a_pair = place(u)
        b_tile, b_pair = place(u - 1)
        c_tile, c_pair = place(u - 2)
        q_a = jnp.concatenate(heads_of(q_ref, a_pair, a_tile), axis=0)
        q_c = jnp.concatenate(heads_of(q_ref, c_pair, c_tile), axis=0)
        b_top = jnp.max(top_ref[...], axis=0, keepdims=True)
        g_c = g_ref[...]
        delta_c = delta_ref[0:1]

        acc_p[:, dim:] += mm_nt(w_ref[top_rows], g_c)
        acc[window(c_tile), dim:] += mm_nt(w_ref[low_rows], g_c)

        tops = []
        for in_prefix, lo, size in chunks:
            at = pl.ds(lo if in_prefix else prefix + lo, size)
            if in_prefix:
                keys, values = pfx[pl.ds(lo, size), :dim], pfx[pl.ds(lo, size), dim:]
            else:
                keys = win[window(a_tile, lo, size), :dim]
                values = win[window(c_tile, lo, size), dim:]
            dp = mm(values, g_c) - delta_c
            d_ref[at] = (w_ref[at].astype(F32) * dp).astype(BF16)
            w_ref[at] = jnp.exp2((s_ref[at] - b_top) * step_scale).astype(BF16)
            score = mm_nt(keys, q_a)
            if not in_prefix:
                score = score + jnp.concatenate([bias[pl.ds(lo, size)]] * PAIR, axis=1)
            s_ref[at] = score
            tops.append(jnp.max(score.reshape(-1, 8, width), axis=0))
        top_ref[...] = functools.reduce(jnp.maximum, tops)

        mixed = mm(pfx_vt[...], w_ref[top_rows])
        mixed = mixed + mm(win_vt[:, window(b_tile)], w_ref[low_rows])
        gq_t = mm(pfx_kt[...], d_ref[top_rows])
        gq_t = gq_t + mm(win_kt[:, window(c_tile)], d_ref[low_rows])
        acc_p[:, :dim] += mm(d_ref[top_rows], q_c)
        acc[window(c_tile), :dim] += mm(d_ref[low_rows], q_c)

        counted = jnp.where((slots_of(b_tile) < ends[-1]) & (u >= 1), F32(1), F32(0))
        inverse = jnp.concatenate([counted] * PAIR, axis=1) / mixed[dim : dim + 1]
        att_t = (mixed[:dim] * inverse).astype(BF16)
        up_t = jnp.concatenate([v.T for v in heads_of(up_ref, b_pair, b_tile)], axis=1)
        g_t = (up_t.astype(F32) * inverse).astype(BF16)
        g_ref[...] = g_t
        delta_ref[0:1] = jnp.sum(g_t.astype(F32) * att_t.astype(F32), axis=0, keepdims=True)
        put_heads(att, b_pair, b_tile, att_t)
        put_heads(gq, c_pair, c_tile, (gq_t * (factor2 * scale)).astype(BF16))

    def give_back(j):
        ret_out[part(j)] = acc[part(j)].astype(BF16)

        @pl.when(has_prev)
        def _():
            ret_copy(j).start()

    def loop_step(u, carry):
        @pl.when((lax.rem(u, pairs) == 0) & (u < units))
        def _():
            set_bias(place(u)[0])

        @pl.when(u == pairs)
        def _():
            for load in other_rows:
                load.wait()

            @pl.when(has_prev)
            def _():
                for j in order[1:]:
                    prev_copy(j).wait_recv()

            pl.loop(0, tiles - 1)(turn)

        for k in range(tiles - 1):

            @pl.when(u == (k + 1) * pairs + 2)
            def _():
                for copy in out_copies(order[k]):
                    copy.start()
                if k >= 1:
                    give_back(k - 1)

        pipeline_step(u)
        return carry

    lax.fori_loop(0, units + 2, loop_step, 0)

    for copy in out_copies(order[-1]):
        copy.start()
    gp_out[...] = acc_p[...].astype(BF16)
    for d, peer in enumerate(seq_peers):
        gp_copy(d, me, peer).start()
    for j in (tiles - 2, tiles - 1):
        give_back(j)

    final = jnp.concatenate([factor * scale, factor], axis=1)
    @pl.loop(0, tiles)
    def _(j):
        @pl.when(has_next)
        def _():
            pltpu.make_async_remote_copy(
                src_ref=ret_out.at[part(j)],
                dst_ref=ret_in.at[part(j)],
                send_sem=ret_send.at[j],
                recv_sem=ret_recv.at[j],
                device_id=(my_p, me + 1),
                device_id_type=pl.DeviceIdType.MESH,
            ).wait_recv()

        gkv[part(j)] = (acc[part(tiles + j)] + ret_in[part(j)].astype(F32)) * final
    gkv_copy = pltpu.make_async_copy(gkv, gkv_hbm.at[0], last_sem.at[0])
    gkv_copy.start()

    sums = acc_p[own_block]
    for d, peer in enumerate(seq_peers):
        gp_copy(d, peer, me).wait_recv()
        sums = sums + gp_in[peer].astype(F32)
    gpf[...] = sums * final
    gpf_copy = pltpu.make_async_copy(gpf, gpf_hbm.at[0], last_sem.at[1])
    gpf_copy.start()

    for d, peer in enumerate(seq_peers):
        pf_copy(d, me, peer).wait_send()
        gp_copy(d, me, peer).wait_send()
    for d, peer in enumerate(prompt_peers):
        len_copy(d, my_p, peer).wait_send()

    @pl.when(has_next)
    def _():
        for j in order:
            prev_copy(j).wait_send()

    @pl.when(has_prev)
    def _():
        for j in range(tiles):
            ret_copy(j).wait_send()

    for i in range(tiles):
        for copy in out_copies(i):
            copy.wait()
    gkv_copy.wait()
    gpf_copy.wait()


def body(n_prompt, n_seq, queries, resp_kv, prefix_kv, lengths, upstream):
    rows, width = queries.shape[1:]
    dim = resp_kv.shape[2] // 2
    block = prefix_kv.shape[1]
    prefix = block * n_seq
    tiles = rows // TILE
    keys = prefix + rows + TILE
    lanes = PAIR * dim
    pairs = width // lanes
    dma = pltpu.SemaphoreType.DMA
    anywhere = pl.BlockSpec(memory_space=pl.ANY)
    vmem = pltpu.VMEM
    out_shape = (
        jax.ShapeDtypeStruct(queries.shape, BF16),
        jax.ShapeDtypeStruct(queries.shape, BF16),
        jax.ShapeDtypeStruct(resp_kv.shape, F32),
        jax.ShapeDtypeStruct(prefix_kv.shape, F32),
    )
    placed = [
        pltpu.with_memory_space_constraint(x, pltpu.HBM)
        for x in (lengths, queries, resp_kv, prefix_kv, upstream)
    ]
    return pl.pallas_call(
        functools.partial(kernel, n_prompt, n_seq),
        out_shape=out_shape,
        in_specs=[pl.BlockSpec(memory_space=pltpu.SMEM)] + [pl.BlockSpec(memory_space=pltpu.HBM)] * 4,
        out_specs=(anywhere,) * 4,
        scratch_shapes=[
            vmem((pairs, rows, lanes), BF16),
            vmem((pairs, rows, lanes), BF16),
            vmem((2 * rows, 2 * dim), BF16),
            vmem((prefix, 2 * dim), BF16),
            vmem((dim, 2 * rows), BF16),
            vmem((dim + ONES, 2 * rows), BF16),
            vmem((dim, prefix), BF16),
            vmem((dim + ONES, prefix), BF16),
            vmem((rows + TILE, TILE), F32),
            vmem((keys, lanes), F32),
            vmem((8, lanes), F32),
            vmem((keys, lanes), BF16),
            vmem((dim, lanes), BF16),
            vmem((8, lanes), F32),
            vmem((keys, lanes), BF16),
            vmem((pairs, rows, lanes), BF16),
            vmem((pairs, rows, lanes), BF16),
            vmem((2 * rows, 2 * dim), F32),
            vmem((prefix, 2 * dim), F32),
            vmem((rows, 2 * dim), BF16),
            vmem((rows, 2 * dim), BF16),
            vmem((prefix, 2 * dim), BF16),
            vmem((n_seq, block, 2 * dim), BF16),
            vmem((rows, 2 * dim), F32),
            vmem((block, 2 * dim), F32),
            vmem((n_prompt, 8, 128), F32),
            dma((2,)),
            dma((2, pairs, 2)),
            dma((tiles, pairs, 2)),
            dma((2,)),
            dma((n_seq,)),
            dma((n_seq,)),
            dma((tiles,)),
            dma((tiles,)),
            dma((n_prompt,)),
            dma((n_prompt,)),
            dma((tiles,)),
            dma((tiles,)),
            dma((n_seq,)),
            dma((n_seq,)),
        ],
        compiler_params=pltpu.CompilerParams(
            collective_id=0, has_side_effects=True, vmem_limit_bytes=50 * 1024 * 1024
        ),
        name="attention_core",
    )(*placed)


def solution(mesh):
    spec = P("prompt", "seq", None)
    return jax.shard_map(
        functools.partial(body, mesh.shape["prompt"], mesh.shape["seq"]),
        mesh=mesh,
        in_specs=(spec, spec, spec, P("prompt", None), spec),
        out_specs=(spec, spec, spec, spec),
        check_vma=False,
    )
```

```python
import functools
import math

import jax
import jax.numpy as jnp
from jax import lax
from jax.experimental import pallas as pl
from jax.experimental.pallas import tpu as pltpu
from jax.sharding import PartitionSpec as P

F32 = jnp.float32
BF16 = jnp.bfloat16
TILE = 128
HIDDEN = -1e30
PAIR = 2
CHUNK = 256
ONES = 16


def mm(a, b):
    return lax.dot_general(a, b, (((1,), (0,)), ((), ())), preferred_element_type=F32)


def mm_nt(a, b):
    return lax.dot_general(a, b, (((1,), (1,)), ((), ())), preferred_element_type=F32)


def clear(ref, size):
    @pl.loop(0, size // 64)
    def _(j):
        at = pl.ds(pl.multiple_of(j * 64, 64), 64)
        ref[at] = jnp.zeros((64,) + ref.shape[1:], ref.dtype)


def kernel(
    n_prompt,
    n_seq,
    lens_ref,
    q_hbm,
    kv_hbm,
    pkv_hbm,
    up_hbm,
    att_hbm,
    gq_hbm,
    gkv_hbm,
    gpf_hbm,
    q_ref,
    up_ref,
    win,
    pfx,
    win_kt,
    win_vt,
    pfx_kt,
    pfx_vt,
    bias,
    s_ref,
    top_ref,
    w_ref,
    g_ref,
    delta_ref,
    d_ref,
    att,
    gq,
    acc,
    acc_p,
    ret_out,
    ret_in,
    gp_out,
    gp_in,
    gkv,
    gpf,
    lens_all,
    own_sem,
    in_sem,
    out_sem,
    last_sem,
    pf_send,
    pf_recv,
    prev_send,
    prev_recv,
    len_send,
    len_recv,
    ret_send,
    ret_recv,
    gp_send,
    gp_recv,
):
    pairs, rows, width = q_ref.shape
    dim = win.shape[1] // 2
    tiles = rows // TILE
    block = pkv_hbm.shape[1]
    prefix = pfx.shape[0]
    span = rows + TILE
    responses = lens_ref.shape[1]
    scale = dim ** (-0.5)
    my_p = lax.axis_index("prompt")
    me = lax.axis_index("seq")
    has_next = me < n_seq - 1
    has_prev = me > 0

    seq_peers = [lax.rem(me + d, n_seq) for d in range(1, n_seq)]
    prompt_peers = [lax.rem(my_p + d, n_prompt) for d in range(1, n_prompt)]

    barrier = pltpu.get_barrier_semaphore()
    for peer in seq_peers:
        pl.semaphore_signal(
            barrier, inc=1, device_id=(my_p, peer), device_id_type=pl.DeviceIdType.MESH
        )
    for peer in prompt_peers:
        pl.semaphore_signal(
            barrier, inc=1, device_id=(peer, me), device_id_type=pl.DeviceIdType.MESH
        )

    own_block = pl.ds(pl.multiple_of(me * block, 16), block)
    loads = [
        pltpu.make_async_copy(kv_hbm.at[0], win.at[pl.ds(rows, rows)], own_sem.at[0]),
        pltpu.make_async_copy(pkv_hbm.at[0], pfx.at[own_block], own_sem.at[1]),
    ]

    def row_loads(some, group):
        copies = []
        for pair in range(pairs):
            lanes = pl.ds(pair * width, width)
            for k, (source, target) in enumerate(((q_hbm, q_ref), (up_hbm, up_ref))):
                copies.append(
                    pltpu.make_async_copy(
                        source.at[0, some, lanes], target.at[pair, some], in_sem.at[group, pair, k]
                    )
                )
        return copies

    order = [tiles - 1] + list(range(tiles - 1))
    early_rows = row_loads(pl.ds((tiles - 1) * TILE, TILE), 0)
    other_rows = row_loads(pl.ds(0, (tiles - 1) * TILE), 1)
    for load in loads + early_rows + other_rows:
        load.start()

    for ref in (top_ref, g_ref, delta_ref):
        ref[...] = jnp.zeros_like(ref)
    clear(s_ref, s_ref.shape[0])
    clear(w_ref, w_ref.shape[0])

    total = lens_ref[0, 0]
    for r in range(1, responses):
        total = total + lens_ref[0, r]
    lens_all[my_p] = jnp.full((8, 128), total, jnp.int32).astype(F32)

    pl.semaphore_wait(barrier, n_seq - 1 + n_prompt - 1)

    def remote(src, dst, send, recv, target):
        return pltpu.make_async_remote_copy(
            src_ref=src,
            dst_ref=dst,
            send_sem=send,
            recv_sem=recv,
            device_id=target,
            device_id_type=pl.DeviceIdType.MESH,
        )

    def part(j):
        return pl.ds(pl.multiple_of(j * TILE, TILE), TILE)

    def prev_copy(j):
        return remote(
            kv_hbm.at[0, part(j)],
            win.at[part(j)],
            prev_send.at[j],
            prev_recv.at[j],
            (my_p, me + 1),
        )

    def ret_copy(j):
        return remote(
            ret_out.at[part(j)],
            ret_in.at[part(j)],
            ret_send.at[j],
            ret_recv.at[j],
            (my_p, me - 1),
        )

    def pf_copy(d, sender, target):
        rows_of = pl.ds(pl.multiple_of(sender * block, 16), block)
        return remote(
            pkv_hbm.at[0], pfx.at[rows_of], pf_send.at[d], pf_recv.at[sender], (my_p, target)
        )

    def len_copy(d, sender, target):
        return remote(
            lens_all.at[sender],
            lens_all.at[sender],
            len_send.at[d],
            len_recv.at[sender],
            (target, me),
        )

    def gp_copy(d, sender, target):
        rows_of = pl.ds(pl.multiple_of(target * block, 16), block)
        return remote(
            gp_out.at[rows_of],
            gp_in.at[sender],
            gp_send.at[d],
            gp_recv.at[sender],
            (my_p, target),
        )

    for d, peer in enumerate(seq_peers):
        pf_copy(d, me, peer).start()

    @pl.when(has_next)
    def _():
        prev_copy(order[0]).start()

    for d, peer in enumerate(prompt_peers):
        len_copy(d, my_p, peer).start()

    @pl.when(has_next)
    def _():
        for j in order[1:]:
            prev_copy(j).start()

    @pl.when(jnp.logical_not(has_prev))
    def _():
        clear(win, rows)

    @pl.when(jnp.logical_not(has_next))
    def _():
        clear(ret_in, rows)

    clear(acc, 2 * rows)
    clear(acc_p, prefix)
    win_vt[pl.ds(dim, ONES)] = jnp.ones((ONES, 2 * rows), BF16)
    pfx_vt[pl.ds(dim, ONES)] = jnp.ones((ONES, pfx.shape[0]), BF16)

    def turn(j):
        keys = win[part(j), :dim]
        values = win[part(j), dim:]
        win_kt[:, part(j)] = keys.T
        win_vt[pl.ds(0, dim), part(j)] = values.T

    loads[0].wait()
    pl.loop(tiles, 2 * tiles)(turn)
    for load in loads[1:] + early_rows:
        load.wait()
    for d, peer in enumerate(seq_peers):
        pf_copy(d, peer, me).wait_recv()
    pfx_kt[...] = pfx[:, :dim].T
    pfx_vt[pl.ds(0, dim)] = pfx[:, dim:].T

    @pl.when(has_prev)
    def _():
        prev_copy(order[0]).wait_recv()

    turn(order[0])
    for d, peer in enumerate(prompt_peers):
        len_copy(d, peer, my_p).wait_recv()
    tokens = lens_all[0]
    for p in range(1, n_prompt):
        tokens = tokens + lens_all[p]
    factor = (F32(n_prompt * n_seq * rows) / tokens)[:1]
    factor2 = jnp.concatenate([factor] * PAIR, axis=1)

    ends = []
    for r in range(responses):
        ends.append(lens_ref[0, r] + (ends[-1] if ends else 0))
    units = tiles * pairs
    step_scale = scale * math.log2(math.e)

    def out_copies(i):
        copies = []
        for pair in range(pairs):
            lanes = pl.ds(pair * width, width)
            for which, (source, target) in enumerate(((att, att_hbm), (gq, gq_hbm))):
                copies.append(
                    pltpu.make_async_copy(
                        source.at[pair, tile_rows(i)],
                        target.at[0, tile_rows(i), lanes],
                        out_sem.at[i, pair, which],
                    )
                )
        return copies

    def tile_rows(i):
        return pl.ds(pl.multiple_of(i * TILE, TILE), TILE)

    def place(unit):
        unit = jnp.clip(unit, 0, units - 1)
        i = lax.rem(lax.div(unit, pairs) + tiles - 1, tiles)
        return i, lax.rem(unit, pairs)

    def slots_of(i):
        return me * rows + i * TILE + lax.broadcasted_iota(jnp.int32, (1, TILE), 1)

    def set_bias(i):
        slots = slots_of(i)
        first = jnp.zeros((1, TILE), jnp.int32)
        for end in ends:
            first = jnp.where(slots >= end, end, first)
        key_slots = (me - 1) * rows + i * TILE + lax.broadcasted_iota(jnp.int32, (span, TILE), 0)
        seen = (key_slots >= first) & (key_slots <= slots)
        bias[...] = jnp.where(seen, F32(0), F32(HIDDEN))

    def heads_of(ref, pair, i):
        return [ref[pair, tile_rows(i), k * dim : (k + 1) * dim] for k in range(PAIR)]

    def put_heads(ref, pair, i, value_t):
        for k in range(PAIR):
            ref[pair, tile_rows(i), k * dim : (k + 1) * dim] = value_t[
                :, k * TILE : (k + 1) * TILE
            ].T

    def window(i, lo=0, size=span):
        return pl.ds(pl.multiple_of(i * TILE + lo, TILE), size)

    low_rows, top_rows = pl.ds(prefix, span), pl.ds(0, prefix)
    chunks = [(True, lo, min(CHUNK, prefix - lo)) for lo in range(0, prefix, CHUNK)]
    chunks += [(False, lo, min(CHUNK, span - lo)) for lo in range(0, span, CHUNK)]

    def pipeline_step(u):
        a_tile, a_pair = place(u)
        b_tile, b_pair = place(u - 1)
        c_tile, c_pair = place(u - 2)
        q_a = jnp.concatenate(heads_of(q_ref, a_pair, a_tile), axis=0)
        q_c = jnp.concatenate(heads_of(q_ref, c_pair, c_tile), axis=0)
        b_top = jnp.max(top_ref[...], axis=0, keepdims=True)
        g_c = g_ref[...]
        delta_c = delta_ref[0:1]

        acc_p[:, dim:] += mm_nt(w_ref[top_rows], g_c)
        acc[window(c_tile), dim:] += mm_nt(w_ref[low_rows], g_c)

        tops = []
        for in_prefix, lo, size in chunks:
            at = pl.ds(lo if in_prefix else prefix + lo, size)
            if in_prefix:
                keys, values = pfx[pl.ds(lo, size), :dim], pfx[pl.ds(lo, size), dim:]
            else:
                keys = win[window(a_tile, lo, size), :dim]
                values = win[window(c_tile, lo, size), dim:]
            dp = mm(values, g_c) - delta_c
            d_ref[at] = (w_ref[at].astype(F32) * dp).astype(BF16)
            w_ref[at] = jnp.exp2((s_ref[at] - b_top) * step_scale).astype(BF16)
            score = mm_nt(keys, q_a)
            if not in_prefix:
                score = score + jnp.concatenate([bias[pl.ds(lo, size)]] * PAIR, axis=1)
            s_ref[at] = score
            tops.append(jnp.max(score.reshape(-1, 8, width), axis=0))
        top_ref[...] = functools.reduce(jnp.maximum, tops)

        mixed = mm(pfx_vt[...], w_ref[top_rows])
        mixed = mixed + mm(win_vt[:, window(b_tile)], w_ref[low_rows])
        gq_t = mm(pfx_kt[...], d_ref[top_rows])
        gq_t = gq_t + mm(win_kt[:, window(c_tile)], d_ref[low_rows])
        acc_p[:, :dim] += mm(d_ref[top_rows], q_c)
        acc[window(c_tile), :dim] += mm(d_ref[low_rows], q_c)

        counted = jnp.where((slots_of(b_tile) < ends[-1]) & (u >= 1), F32(1), F32(0))
        inverse = jnp.concatenate([counted] * PAIR, axis=1) / mixed[dim : dim + 1]
        att_t = (mixed[:dim] * inverse).astype(BF16)
        up_t = jnp.concatenate([v.T for v in heads_of(up_ref, b_pair, b_tile)], axis=1)
        g_t = (up_t.astype(F32) * inverse).astype(BF16)
        g_ref[...] = g_t
        delta_ref[0:1] = jnp.sum(g_t.astype(F32) * att_t.astype(F32), axis=0, keepdims=True)
        put_heads(att, b_pair, b_tile, att_t)
        put_heads(gq, c_pair, c_tile, (gq_t * (factor2 * scale)).astype(BF16))

    def give_back(j):
        ret_out[part(j)] = acc[part(j)].astype(BF16)

        @pl.when(has_prev)
        def _():
            ret_copy(j).start()

    def loop_step(u, carry):
        @pl.when((lax.rem(u, pairs) == 0) & (u < units))
        def _():
            set_bias(place(u)[0])

        @pl.when(u == pairs)
        def _():
            for load in other_rows:
                load.wait()

            @pl.when(has_prev)
            def _():
                for j in order[1:]:
                    prev_copy(j).wait_recv()

            pl.loop(0, tiles - 1)(turn)

        for k in range(tiles - 1):

            @pl.when(u == (k + 1) * pairs + 2)
            def _():
                for copy in out_copies(order[k]):
                    copy.start()
                if k >= 1:
                    give_back(k - 1)

        pipeline_step(u)
        return carry

    lax.fori_loop(0, units + 2, loop_step, 0)

    for copy in out_copies(order[-1]):
        copy.start()
    gp_out[...] = acc_p[...].astype(BF16)
    for d, peer in enumerate(seq_peers):
        gp_copy(d, me, peer).start()
    for j in (tiles - 2, tiles - 1):
        give_back(j)

    final = jnp.concatenate([factor * scale, factor], axis=1)
    @pl.loop(0, tiles)
    def _(j):
        @pl.when(has_next)
        def _():
            pltpu.make_async_remote_copy(
                src_ref=ret_out.at[part(j)],
                dst_ref=ret_in.at[part(j)],
                send_sem=ret_send.at[j],
                recv_sem=ret_recv.at[j],
                device_id=(my_p, me + 1),
                device_id_type=pl.DeviceIdType.MESH,
            ).wait_recv()

        gkv[part(j)] = (acc[part(tiles + j)] + ret_in[part(j)].astype(F32)) * final
    gkv_copy = pltpu.make_async_copy(gkv, gkv_hbm.at[0], last_sem.at[0])
    gkv_copy.start()

    sums = acc_p[own_block]
    for d, peer in enumerate(seq_peers):
        gp_copy(d, peer, me).wait_recv()
        sums = sums + gp_in[peer].astype(F32)
    gpf[...] = sums * final
    gpf_copy = pltpu.make_async_copy(gpf, gpf_hbm.at[0], last_sem.at[1])
    gpf_copy.start()

    for d, peer in enumerate(seq_peers):
        pf_copy(d, me, peer).wait_send()
        gp_copy(d, me, peer).wait_send()
    for d, peer in enumerate(prompt_peers):
        len_copy(d, my_p, peer).wait_send()

    @pl.when(has_next)
    def _():
        for j in order:
            prev_copy(j).wait_send()

    @pl.when(has_prev)
    def _():
        for j in range(tiles):
            ret_copy(j).wait_send()

    for i in range(tiles):
        for copy in out_copies(i):
            copy.wait()
    gkv_copy.wait()
    gpf_copy.wait()


def body(n_prompt, n_seq, queries, resp_kv, prefix_kv, lengths, upstream):
    rows, width = queries.shape[1:]
    dim = resp_kv.shape[2] // 2
    block = prefix_kv.shape[1]
    prefix = block * n_seq
    tiles = rows // TILE
    keys = prefix + rows + TILE
    lanes = PAIR * dim
    pairs = width // lanes
    dma = pltpu.SemaphoreType.DMA
    anywhere = pl.BlockSpec(memory_space=pl.ANY)
    vmem = pltpu.VMEM
    out_shape = (
        jax.ShapeDtypeStruct(queries.shape, BF16),
        jax.ShapeDtypeStruct(queries.shape, BF16),
        jax.ShapeDtypeStruct(resp_kv.shape, F32),
        jax.ShapeDtypeStruct(prefix_kv.shape, F32),
    )
    placed = [
        pltpu.with_memory_space_constraint(x, pltpu.HBM)
        for x in (lengths, queries, resp_kv, prefix_kv, upstream)
    ]
    return pl.pallas_call(
        functools.partial(kernel, n_prompt, n_seq),
        out_shape=out_shape,
        in_specs=[pl.BlockSpec(memory_space=pltpu.SMEM)] + [pl.BlockSpec(memory_space=pltpu.HBM)] * 4,
        out_specs=(anywhere,) * 4,
        scratch_shapes=[
            vmem((pairs, rows, lanes), BF16),
            vmem((pairs, rows, lanes), BF16),
            vmem((2 * rows, 2 * dim), BF16),
            vmem((prefix, 2 * dim), BF16),
            vmem((dim, 2 * rows), BF16),
            vmem((dim + ONES, 2 * rows), BF16),
            vmem((dim, prefix), BF16),
            vmem((dim + ONES, prefix), BF16),
            vmem((rows + TILE, TILE), F32),
            vmem((keys, lanes), F32),
            vmem((8, lanes), F32),
            vmem((keys, lanes), BF16),
            vmem((dim, lanes), BF16),
            vmem((8, lanes), F32),
            vmem((keys, lanes), BF16),
            vmem((pairs, rows, lanes), BF16),
            vmem((pairs, rows, lanes), BF16),
            vmem((2 * rows, 2 * dim), F32),
            vmem((prefix, 2 * dim), F32),
            vmem((rows, 2 * dim), BF16),
            vmem((rows, 2 * dim), BF16),
            vmem((prefix, 2 * dim), BF16),
            vmem((n_seq, block, 2 * dim), BF16),
            vmem((rows, 2 * dim), F32),
            vmem((block, 2 * dim), F32),
            vmem((n_prompt, 8, 128), F32),
            dma((2,)),
            dma((2, pairs, 2)),
            dma((tiles, pairs, 2)),
            dma((2,)),
            dma((n_seq,)),
            dma((n_seq,)),
            dma((tiles,)),
            dma((tiles,)),
            dma((n_prompt,)),
            dma((n_prompt,)),
            dma((tiles,)),
            dma((tiles,)),
            dma((n_seq,)),
            dma((n_seq,)),
        ],
        compiler_params=pltpu.CompilerParams(
            collective_id=0, has_side_effects=True, vmem_limit_bytes=50 * 1024 * 1024
        ),
        name="attention_core",
    )(*placed)


def solution(mesh):
    spec = P("prompt", "seq", None)
    return jax.shard_map(
        functools.partial(body, mesh.shape["prompt"], mesh.shape["seq"]),
        mesh=mesh,
        in_specs=(spec, spec, spec, P("prompt", None), spec),
        out_specs=(spec, spec, spec, spec),
        check_vma=False,
    )
```

```python
import functools
import math

import jax
import jax.numpy as jnp
from jax import lax
from jax.experimental import pallas as pl
from jax.experimental.pallas import tpu as pltpu
from jax.sharding import PartitionSpec as P

F32 = jnp.float32
BF16 = jnp.bfloat16
TILE = 128
HIDDEN = -1e30
PAIR = 2
CHUNK = 64
ONES = 16


def mm(a, b):
    return lax.dot_general(a, b, (((1,), (0,)), ((), ())), preferred_element_type=F32)


def mm_nt(a, b):
    return lax.dot_general(a, b, (((1,), (1,)), ((), ())), preferred_element_type=F32)


def clear(ref, size):
    @pl.loop(0, size // 64)
    def _(j):
        at = pl.ds(pl.multiple_of(j * 64, 64), 64)
        ref[at] = jnp.zeros((64,) + ref.shape[1:], ref.dtype)


def kernel(
    n_prompt,
    n_seq,
    lens_ref,
    q_hbm,
    kv_hbm,
    pkv_hbm,
    up_hbm,
    att_hbm,
    gq_hbm,
    gkv_hbm,
    gpf_hbm,
    q_ref,
    up_ref,
    win,
    pfx,
    win_kt,
    win_vt,
    pfx_kt,
    pfx_vt,
    bias,
    s_ref,
    top_ref,
    w_ref,
    g_ref,
    delta_ref,
    d_ref,
    att,
    gq,
    acc,
    acc_p,
    ret_out,
    ret_in,
    gp_out,
    gp_in,
    gkv,
    gpf,
    lens_all,
    own_sem,
    in_sem,
    out_sem,
    last_sem,
    pf_send,
    pf_recv,
    prev_send,
    prev_recv,
    len_send,
    len_recv,
    ret_send,
    ret_recv,
    gp_send,
    gp_recv,
):
    pairs, rows, width = q_ref.shape
    dim = win.shape[1] // 2
    tiles = rows // TILE
    block = pkv_hbm.shape[1]
    prefix = pfx.shape[0]
    span = rows + TILE
    responses = lens_ref.shape[1]
    scale = dim ** (-0.5)
    my_p = lax.axis_index("prompt")
    me = lax.axis_index("seq")
    has_next = me < n_seq - 1
    has_prev = me > 0

    seq_peers = [lax.rem(me + d, n_seq) for d in range(1, n_seq)]
    prompt_peers = [lax.rem(my_p + d, n_prompt) for d in range(1, n_prompt)]

    barrier = pltpu.get_barrier_semaphore()
    for peer in seq_peers:
        pl.semaphore_signal(
            barrier, inc=1, device_id=(my_p, peer), device_id_type=pl.DeviceIdType.MESH
        )
    for peer in prompt_peers:
        pl.semaphore_signal(
            barrier, inc=1, device_id=(peer, me), device_id_type=pl.DeviceIdType.MESH
        )

    own_block = pl.ds(pl.multiple_of(me * block, 16), block)
    loads = [
        pltpu.make_async_copy(kv_hbm.at[0], win.at[pl.ds(rows, rows)], own_sem.at[0]),
        pltpu.make_async_copy(pkv_hbm.at[0], pfx.at[own_block], own_sem.at[1]),
    ]

    def row_loads(some, group):
        copies = []
        for pair in range(pairs):
            lanes = pl.ds(pair * width, width)
            for k, (source, target) in enumerate(((q_hbm, q_ref), (up_hbm, up_ref))):
                copies.append(
                    pltpu.make_async_copy(
                        source.at[0, some, lanes], target.at[pair, some], in_sem.at[group, pair, k]
                    )
                )
        return copies

    order = [tiles - 1] + list(range(tiles - 1))
    early_rows = row_loads(pl.ds((tiles - 1) * TILE, TILE), 0)
    other_rows = row_loads(pl.ds(0, (tiles - 1) * TILE), 1)
    for load in loads + early_rows + other_rows:
        load.start()

    for ref in (top_ref, g_ref, delta_ref):
        ref[...] = jnp.zeros_like(ref)
    clear(s_ref, s_ref.shape[0])
    clear(w_ref, w_ref.shape[0])

    total = lens_ref[0, 0]
    for r in range(1, responses):
        total = total + lens_ref[0, r]
    lens_all[my_p] = jnp.full((8, 128), total, jnp.int32).astype(F32)

    pl.semaphore_wait(barrier, n_seq - 1 + n_prompt - 1)

    def remote(src, dst, send, recv, target):
        return pltpu.make_async_remote_copy(
            src_ref=src,
            dst_ref=dst,
            send_sem=send,
            recv_sem=recv,
            device_id=target,
            device_id_type=pl.DeviceIdType.MESH,
        )

    def part(j):
        return pl.ds(pl.multiple_of(j * TILE, TILE), TILE)

    def prev_copy(j):
        return remote(
            kv_hbm.at[0, part(j)],
            win.at[part(j)],
            prev_send.at[j],
            prev_recv.at[j],
            (my_p, me + 1),
        )

    def ret_copy(j):
        return remote(
            ret_out.at[part(j)],
            ret_in.at[part(j)],
            ret_send.at[j],
            ret_recv.at[j],
            (my_p, me - 1),
        )

    def pf_copy(d, sender, target):
        rows_of = pl.ds(pl.multiple_of(sender * block, 16), block)
        return remote(
            pkv_hbm.at[0], pfx.at[rows_of], pf_send.at[d], pf_recv.at[sender], (my_p, target)
        )

    def len_copy(d, sender, target):
        return remote(
            lens_all.at[sender],
            lens_all.at[sender],
            len_send.at[d],
            len_recv.at[sender],
            (target, me),
        )

    def gp_copy(d, sender, target):
        rows_of = pl.ds(pl.multiple_of(target * block, 16), block)
        return remote(
            gp_out.at[rows_of],
            gp_in.at[sender],
            gp_send.at[d],
            gp_recv.at[sender],
            (my_p, target),
        )

    for d, peer in enumerate(seq_peers):
        pf_copy(d, me, peer).start()

    @pl.when(has_next)
    def _():
        prev_copy(order[0]).start()

    for d, peer in enumerate(prompt_peers):
        len_copy(d, my_p, peer).start()

    @pl.when(has_next)
    def _():
        for j in order[1:]:
            prev_copy(j).start()

    @pl.when(jnp.logical_not(has_prev))
    def _():
        clear(win, rows)

    @pl.when(jnp.logical_not(has_next))
    def _():
        clear(ret_in, rows)

    clear(acc, 2 * rows)
    clear(acc_p, prefix)
    win_vt[pl.ds(dim, ONES)] = jnp.ones((ONES, 2 * rows), BF16)
    pfx_vt[pl.ds(dim, ONES)] = jnp.ones((ONES, pfx.shape[0]), BF16)

    def turn(j):
        keys = win[part(j), :dim]
        values = win[part(j), dim:]
        win_kt[:, part(j)] = keys.T
        win_vt[pl.ds(0, dim), part(j)] = values.T

    loads[0].wait()
    pl.loop(tiles, 2 * tiles)(turn)
    for load in loads[1:] + early_rows:
        load.wait()
    for d, peer in enumerate(seq_peers):
        pf_copy(d, peer, me).wait_recv()
    pfx_kt[...] = pfx[:, :dim].T
    pfx_vt[pl.ds(0, dim)] = pfx[:, dim:].T

    @pl.when(has_prev)
    def _():
        prev_copy(order[0]).wait_recv()

    turn(order[0])
    for d, peer in enumerate(prompt_peers):
        len_copy(d, peer, my_p).wait_recv()
    tokens = lens_all[0]
    for p in range(1, n_prompt):
        tokens = tokens + lens_all[p]
    factor = (F32(n_prompt * n_seq * rows) / tokens)[:1]
    factor2 = jnp.concatenate([factor] * PAIR, axis=1)

    ends = []
    for r in range(responses):
        ends.append(lens_ref[0, r] + (ends[-1] if ends else 0))
    units = tiles * pairs
    step_scale = scale * math.log2(math.e)

    def out_copies(i):
        copies = []
        for pair in range(pairs):
            lanes = pl.ds(pair * width, width)
            for which, (source, target) in enumerate(((att, att_hbm), (gq, gq_hbm))):
                copies.append(
                    pltpu.make_async_copy(
                        source.at[pair, tile_rows(i)],
                        target.at[0, tile_rows(i), lanes],
                        out_sem.at[i, pair, which],
                    )
                )
        return copies

    def tile_rows(i):
        return pl.ds(pl.multiple_of(i * TILE, TILE), TILE)

    def place(unit):
        unit = jnp.clip(unit, 0, units - 1)
        i = lax.rem(lax.div(unit, pairs) + tiles - 1, tiles)
        return i, lax.rem(unit, pairs)

    def slots_of(i):
        return me * rows + i * TILE + lax.broadcasted_iota(jnp.int32, (1, TILE), 1)

    def set_bias(i):
        slots = slots_of(i)
        first = jnp.zeros((1, TILE), jnp.int32)
        for end in ends:
            first = jnp.where(slots >= end, end, first)
        key_slots = (me - 1) * rows + i * TILE + lax.broadcasted_iota(jnp.int32, (span, TILE), 0)
        seen = (key_slots >= first) & (key_slots <= slots)
        bias[...] = jnp.where(seen, F32(0), F32(HIDDEN))

    def heads_of(ref, pair, i):
        return [ref[pair, tile_rows(i), k * dim : (k + 1) * dim] for k in range(PAIR)]

    def put_heads(ref, pair, i, value_t):
        for k in range(PAIR):
            ref[pair, tile_rows(i), k * dim : (k + 1) * dim] = value_t[
                :, k * TILE : (k + 1) * TILE
            ].T

    def window(i, lo=0, size=span):
        return pl.ds(pl.multiple_of(i * TILE + lo, math.gcd(TILE, lo)), size)

    low_rows, top_rows = pl.ds(prefix, span), pl.ds(0, prefix)
    chunks = [(True, lo, min(CHUNK, prefix - lo)) for lo in range(0, prefix, CHUNK)]
    chunks += [(False, lo, min(CHUNK, span - lo)) for lo in range(0, span, CHUNK)]

    def pipeline_step(u):
        a_tile, a_pair = place(u)
        b_tile, b_pair = place(u - 1)
        c_tile, c_pair = place(u - 2)
        q_a = jnp.concatenate(heads_of(q_ref, a_pair, a_tile), axis=0)
        q_c = jnp.concatenate(heads_of(q_ref, c_pair, c_tile), axis=0)
        b_top = jnp.max(top_ref[...], axis=0, keepdims=True)
        g_c = g_ref[...]
        delta_c = delta_ref[0:1]

        acc_p[:, dim:] += mm_nt(w_ref[top_rows], g_c)
        acc[window(c_tile), dim:] += mm_nt(w_ref[low_rows], g_c)

        tops = []
        for in_prefix, lo, size in chunks:
            at = pl.ds(lo if in_prefix else prefix + lo, size)
            if in_prefix:
                keys, values = pfx[pl.ds(lo, size), :dim], pfx[pl.ds(lo, size), dim:]
            else:
                keys = win[window(a_tile, lo, size), :dim]
                values = win[window(c_tile, lo, size), dim:]
            dp = mm(values, g_c) - delta_c
            d_ref[at] = (w_ref[at].astype(F32) * dp).astype(BF16)
            w_ref[at] = jnp.exp2((s_ref[at] - b_top) * step_scale).astype(BF16)
            score = mm_nt(keys, q_a)
            if not in_prefix:
                score = score + jnp.concatenate([bias[pl.ds(lo, size)]] * PAIR, axis=1)
            s_ref[at] = score
            tops.append(jnp.max(score.reshape(-1, 8, width), axis=0))
        top_ref[...] = functools.reduce(jnp.maximum, tops)

        mixed = mm(pfx_vt[...], w_ref[top_rows])
        mixed = mixed + mm(win_vt[:, window(b_tile)], w_ref[low_rows])
        gq_t = mm(pfx_kt[...], d_ref[top_rows])
        gq_t = gq_t + mm(win_kt[:, window(c_tile)], d_ref[low_rows])
        acc_p[:, :dim] += mm(d_ref[top_rows], q_c)
        acc[window(c_tile), :dim] += mm(d_ref[low_rows], q_c)

        counted = jnp.where((slots_of(b_tile) < ends[-1]) & (u >= 1), F32(1), F32(0))
        inverse = jnp.concatenate([counted] * PAIR, axis=1) / mixed[dim : dim + 1]
        att_t = (mixed[:dim] * inverse).astype(BF16)
        up_t = jnp.concatenate([v.T for v in heads_of(up_ref, b_pair, b_tile)], axis=1)
        g_t = (up_t.astype(F32) * inverse).astype(BF16)
        g_ref[...] = g_t
        delta_ref[0:1] = jnp.sum(g_t.astype(F32) * att_t.astype(F32), axis=0, keepdims=True)
        put_heads(att, b_pair, b_tile, att_t)
        put_heads(gq, c_pair, c_tile, (gq_t * (factor2 * scale)).astype(BF16))

    def give_back(j):
        ret_out[part(j)] = acc[part(j)].astype(BF16)

        @pl.when(has_prev)
        def _():
            ret_copy(j).start()

    def loop_step(u, carry):
        @pl.when((lax.rem(u, pairs) == 0) & (u < units))
        def _():
            set_bias(place(u)[0])

        @pl.when(u == pairs)
        def _():
            for load in other_rows:
                load.wait()

            @pl.when(has_prev)
            def _():
                for j in order[1:]:
                    prev_copy(j).wait_recv()

            pl.loop(0, tiles - 1)(turn)

        for k in range(tiles - 1):

            @pl.when(u == (k + 1) * pairs + 2)
            def _():
                for copy in out_copies(order[k]):
                    copy.start()
                if k >= 1:
                    give_back(k - 1)

        pipeline_step(u)
        return carry

    lax.fori_loop(0, units + 2, loop_step, 0)

    for copy in out_copies(order[-1]):
        copy.start()
    gp_out[...] = acc_p[...].astype(BF16)
    for d, peer in enumerate(seq_peers):
        gp_copy(d, me, peer).start()
    for j in (tiles - 2, tiles - 1):
        give_back(j)

    final = jnp.concatenate([factor * scale, factor], axis=1)
    @pl.loop(0, tiles)
    def _(j):
        @pl.when(has_next)
        def _():
            pltpu.make_async_remote_copy(
                src_ref=ret_out.at[part(j)],
                dst_ref=ret_in.at[part(j)],
                send_sem=ret_send.at[j],
                recv_sem=ret_recv.at[j],
                device_id=(my_p, me + 1),
                device_id_type=pl.DeviceIdType.MESH,
            ).wait_recv()

        gkv[part(j)] = (acc[part(tiles + j)] + ret_in[part(j)].astype(F32)) * final
    gkv_copy = pltpu.make_async_copy(gkv, gkv_hbm.at[0], last_sem.at[0])
    gkv_copy.start()

    sums = acc_p[own_block]
    for d, peer in enumerate(seq_peers):
        gp_copy(d, peer, me).wait_recv()
        sums = sums + gp_in[peer].astype(F32)
    gpf[...] = sums * final
    gpf_copy = pltpu.make_async_copy(gpf, gpf_hbm.at[0], last_sem.at[1])
    gpf_copy.start()

    for d, peer in enumerate(seq_peers):
        pf_copy(d, me, peer).wait_send()
        gp_copy(d, me, peer).wait_send()
    for d, peer in enumerate(prompt_peers):
        len_copy(d, my_p, peer).wait_send()

    @pl.when(has_next)
    def _():
        for j in order:
            prev_copy(j).wait_send()

    @pl.when(has_prev)
    def _():
        for j in range(tiles):
            ret_copy(j).wait_send()

    for i in range(tiles):
        for copy in out_copies(i):
            copy.wait()
    gkv_copy.wait()
    gpf_copy.wait()


def body(n_prompt, n_seq, queries, resp_kv, prefix_kv, lengths, upstream):
    rows, width = queries.shape[1:]
    dim = resp_kv.shape[2] // 2
    block = prefix_kv.shape[1]
    prefix = block * n_seq
    tiles = rows // TILE
    keys = prefix + rows + TILE
    lanes = PAIR * dim
    pairs = width // lanes
    dma = pltpu.SemaphoreType.DMA
    anywhere = pl.BlockSpec(memory_space=pl.ANY)
    vmem = pltpu.VMEM
    out_shape = (
        jax.ShapeDtypeStruct(queries.shape, BF16),
        jax.ShapeDtypeStruct(queries.shape, BF16),
        jax.ShapeDtypeStruct(resp_kv.shape, F32),
        jax.ShapeDtypeStruct(prefix_kv.shape, F32),
    )
    placed = [
        pltpu.with_memory_space_constraint(x, pltpu.HBM)
        for x in (lengths, queries, resp_kv, prefix_kv, upstream)
    ]
    return pl.pallas_call(
        functools.partial(kernel, n_prompt, n_seq),
        out_shape=out_shape,
        in_specs=[pl.BlockSpec(memory_space=pltpu.SMEM)] + [pl.BlockSpec(memory_space=pltpu.HBM)] * 4,
        out_specs=(anywhere,) * 4,
        scratch_shapes=[
            vmem((pairs, rows, lanes), BF16),
            vmem((pairs, rows, lanes), BF16),
            vmem((2 * rows, 2 * dim), BF16),
            vmem((prefix, 2 * dim), BF16),
            vmem((dim, 2 * rows), BF16),
            vmem((dim + ONES, 2 * rows), BF16),
            vmem((dim, prefix), BF16),
            vmem((dim + ONES, prefix), BF16),
            vmem((rows + TILE, TILE), F32),
            vmem((keys, lanes), F32),
            vmem((8, lanes), F32),
            vmem((keys, lanes), BF16),
            vmem((dim, lanes), BF16),
            vmem((8, lanes), F32),
            vmem((keys, lanes), BF16),
            vmem((pairs, rows, lanes), BF16),
            vmem((pairs, rows, lanes), BF16),
            vmem((2 * rows, 2 * dim), F32),
            vmem((prefix, 2 * dim), F32),
            vmem((rows, 2 * dim), BF16),
            vmem((rows, 2 * dim), BF16),
            vmem((prefix, 2 * dim), BF16),
            vmem((n_seq, block, 2 * dim), BF16),
            vmem((rows, 2 * dim), F32),
            vmem((block, 2 * dim), F32),
            vmem((n_prompt, 8, 128), F32),
            dma((2,)),
            dma((2, pairs, 2)),
            dma((tiles, pairs, 2)),
            dma((2,)),
            dma((n_seq,)),
            dma((n_seq,)),
            dma((tiles,)),
            dma((tiles,)),
            dma((n_prompt,)),
            dma((n_prompt,)),
            dma((tiles,)),
            dma((tiles,)),
            dma((n_seq,)),
            dma((n_seq,)),
        ],
        compiler_params=pltpu.CompilerParams(
            collective_id=0, has_side_effects=True, vmem_limit_bytes=50 * 1024 * 1024
        ),
        name="attention_core",
    )(*placed)


def solution(mesh):
    spec = P("prompt", "seq", None)
    return jax.shard_map(
        functools.partial(body, mesh.shape["prompt"], mesh.shape["seq"]),
        mesh=mesh,
        in_specs=(spec, spec, spec, P("prompt", None), spec),
        out_specs=(spec, spec, spec, spec),
        check_vma=False,
    )
```

```python
import functools
import math

import jax
import jax.numpy as jnp
from jax import lax
from jax.experimental import pallas as pl
from jax.experimental.pallas import tpu as pltpu
from jax.sharding import PartitionSpec as P

F32 = jnp.float32
BF16 = jnp.bfloat16
TILE = 128
HIDDEN = -1e30
PAIR = 2
CHUNK = 128
ONES = 16


def mm(a, b):
    return lax.dot_general(a, b, (((1,), (0,)), ((), ())), preferred_element_type=F32)


def mm_nt(a, b):
    return lax.dot_general(a, b, (((1,), (1,)), ((), ())), preferred_element_type=F32)


def clear(ref, size):
    @pl.loop(0, size // 64)
    def _(j):
        at = pl.ds(pl.multiple_of(j * 64, 64), 64)
        ref[at] = jnp.zeros((64,) + ref.shape[1:], ref.dtype)


def kernel(
    n_prompt,
    n_seq,
    lens_ref,
    q_hbm,
    kv_hbm,
    pkv_hbm,
    up_hbm,
    att_hbm,
    gq_hbm,
    gkv_hbm,
    gpf_hbm,
    q_ref,
    up_ref,
    win,
    pfx,
    win_kt,
    win_vt,
    pfx_kt,
    pfx_vt,
    bias,
    s_ref,
    top_ref,
    w_ref,
    g_ref,
    delta_ref,
    d_ref,
    att,
    gq,
    acc,
    acc_p,
    ret_out,
    ret_in,
    gp_out,
    gp_in,
    gkv,
    gpf,
    lens_all,
    own_sem,
    in_sem,
    out_sem,
    last_sem,
    pf_send,
    pf_recv,
    prev_send,
    prev_recv,
    len_send,
    len_recv,
    ret_send,
    ret_recv,
    gp_send,
    gp_recv,
):
    pairs, rows, width = q_ref.shape
    dim = win.shape[1] // 2
    tiles = rows // TILE
    block = pkv_hbm.shape[1]
    prefix = pfx.shape[0]
    span = rows + TILE
    responses = lens_ref.shape[1]
    scale = dim ** (-0.5)
    my_p = lax.axis_index("prompt")
    me = lax.axis_index("seq")
    has_next = me < n_seq - 1
    has_prev = me > 0

    seq_peers = [lax.rem(me + d, n_seq) for d in range(1, n_seq)]
    prompt_peers = [lax.rem(my_p + d, n_prompt) for d in range(1, n_prompt)]

    barrier = pltpu.get_barrier_semaphore()
    for peer in seq_peers:
        pl.semaphore_signal(
            barrier, inc=1, device_id=(my_p, peer), device_id_type=pl.DeviceIdType.MESH
        )
    for peer in prompt_peers:
        pl.semaphore_signal(
            barrier, inc=1, device_id=(peer, me), device_id_type=pl.DeviceIdType.MESH
        )

    own_block = pl.ds(pl.multiple_of(me * block, 16), block)
    loads = [
        pltpu.make_async_copy(kv_hbm.at[0], win.at[pl.ds(rows, rows)], own_sem.at[0]),
        pltpu.make_async_copy(pkv_hbm.at[0], pfx.at[own_block], own_sem.at[1]),
    ]

    def row_loads(some, group):
        copies = []
        for pair in range(pairs):
            lanes = pl.ds(pair * width, width)
            for k, (source, target) in enumerate(((q_hbm, q_ref), (up_hbm, up_ref))):
                copies.append(
                    pltpu.make_async_copy(
                        source.at[0, some, lanes], target.at[pair, some], in_sem.at[group, pair, k]
                    )
                )
        return copies

    order = [tiles - 1] + list(range(tiles - 1))
    early_rows = row_loads(pl.ds((tiles - 1) * TILE, TILE), 0)
    other_rows = row_loads(pl.ds(0, (tiles - 1) * TILE), 1)
    for load in loads + early_rows + other_rows:
        load.start()

    for ref in (top_ref, g_ref, delta_ref):
        ref[...] = jnp.zeros_like(ref)
    clear(s_ref, s_ref.shape[0])
    clear(w_ref, w_ref.shape[0])

    total = lens_ref[0, 0]
    for r in range(1, responses):
        total = total + lens_ref[0, r]
    lens_all[my_p] = jnp.full((8, 128), total, jnp.int32).astype(F32)

    pl.semaphore_wait(barrier, n_seq - 1 + n_prompt - 1)

    def remote(src, dst, send, recv, target):
        return pltpu.make_async_remote_copy(
            src_ref=src,
            dst_ref=dst,
            send_sem=send,
            recv_sem=recv,
            device_id=target,
            device_id_type=pl.DeviceIdType.MESH,
        )

    def part(j):
        return pl.ds(pl.multiple_of(j * TILE, TILE), TILE)

    def prev_copy(j):
        return remote(
            kv_hbm.at[0, part(j)],
            win.at[part(j)],
            prev_send.at[j],
            prev_recv.at[j],
            (my_p, me + 1),
        )

    def ret_copy(j):
        return remote(
            ret_out.at[part(j)],
            ret_in.at[part(j)],
            ret_send.at[j],
            ret_recv.at[j],
            (my_p, me - 1),
        )

    def pf_copy(d, sender, target):
        rows_of = pl.ds(pl.multiple_of(sender * block, 16), block)
        return remote(
            pkv_hbm.at[0], pfx.at[rows_of], pf_send.at[d], pf_recv.at[sender], (my_p, target)
        )

    def len_copy(d, sender, target):
        return remote(
            lens_all.at[sender],
            lens_all.at[sender],
            len_send.at[d],
            len_recv.at[sender],
            (target, me),
        )

    def gp_copy(d, sender, target):
        rows_of = pl.ds(pl.multiple_of(target * block, 16), block)
        return remote(
            gp_out.at[rows_of],
            gp_in.at[sender],
            gp_send.at[d],
            gp_recv.at[sender],
            (my_p, target),
        )

    for d, peer in enumerate(seq_peers):
        pf_copy(d, me, peer).start()

    @pl.when(has_next)
    def _():
        prev_copy(order[0]).start()

    for d, peer in enumerate(prompt_peers):
        len_copy(d, my_p, peer).start()

    @pl.when(has_next)
    def _():
        for j in order[1:]:
            prev_copy(j).start()

    @pl.when(jnp.logical_not(has_prev))
    def _():
        clear(win, rows)

    @pl.when(jnp.logical_not(has_next))
    def _():
        clear(ret_in, rows)

    clear(acc, 2 * rows)
    clear(acc_p, prefix)
    win_vt[pl.ds(dim, ONES)] = jnp.ones((ONES, 2 * rows), BF16)
    pfx_vt[pl.ds(dim, ONES)] = jnp.ones((ONES, pfx.shape[0]), BF16)

    def turn(j):
        keys = win[part(j), :dim]
        values = win[part(j), dim:]
        win_kt[:, part(j)] = keys.T
        win_vt[pl.ds(0, dim), part(j)] = values.T

    loads[0].wait()
    pl.loop(tiles, 2 * tiles)(turn)
    for load in loads[1:] + early_rows:
        load.wait()
    for d, peer in enumerate(seq_peers):
        pf_copy(d, peer, me).wait_recv()
    pfx_kt[...] = pfx[:, :dim].T
    pfx_vt[pl.ds(0, dim)] = pfx[:, dim:].T

    @pl.when(has_prev)
    def _():
        prev_copy(order[0]).wait_recv()

    turn(order[0])
    for d, peer in enumerate(prompt_peers):
        len_copy(d, peer, my_p).wait_recv()
    tokens = lens_all[0]
    for p in range(1, n_prompt):
        tokens = tokens + lens_all[p]
    factor = (F32(n_prompt * n_seq * rows) / tokens)[:1]
    factor2 = jnp.concatenate([factor] * PAIR, axis=1)

    ends = []
    for r in range(responses):
        ends.append(lens_ref[0, r] + (ends[-1] if ends else 0))
    units = tiles * pairs
    step_scale = scale * math.log2(math.e)

    def out_copies(i):
        copies = []
        for pair in range(pairs):
            lanes = pl.ds(pair * width, width)
            for which, (source, target) in enumerate(((att, att_hbm), (gq, gq_hbm))):
                copies.append(
                    pltpu.make_async_copy(
                        source.at[pair, tile_rows(i)],
                        target.at[0, tile_rows(i), lanes],
                        out_sem.at[i, pair, which],
                    )
                )
        return copies

    def tile_rows(i):
        return pl.ds(pl.multiple_of(i * TILE, TILE), TILE)

    def place(unit):
        unit = jnp.clip(unit, 0, units - 1)
        i = lax.rem(lax.div(unit, pairs) + tiles - 1, tiles)
        return i, lax.rem(unit, pairs)

    def slots_of(i):
        return me * rows + i * TILE + lax.broadcasted_iota(jnp.int32, (1, TILE), 1)

    def set_bias(i):
        slots = slots_of(i)
        first = jnp.zeros((1, TILE), jnp.int32)
        for end in ends:
            first = jnp.where(slots >= end, end, first)
        key_slots = (me - 1) * rows + i * TILE + lax.broadcasted_iota(jnp.int32, (span, TILE), 0)
        seen = (key_slots >= first) & (key_slots <= slots)
        bias[...] = jnp.where(seen, F32(0), F32(HIDDEN))

    def heads_of(ref, pair, i):
        return [ref[pair, tile_rows(i), k * dim : (k + 1) * dim] for k in range(PAIR)]

    def put_heads(ref, pair, i, value_t):
        for k in range(PAIR):
            ref[pair, tile_rows(i), k * dim : (k + 1) * dim] = value_t[
                :, k * TILE : (k + 1) * TILE
            ].T

    def window(i, lo=0, size=span):
        return pl.ds(pl.multiple_of(i * TILE + lo, math.gcd(TILE, lo)), size)

    low_rows, top_rows = pl.ds(prefix, span), pl.ds(0, prefix)
    first_size = CHUNK + prefix % CHUNK
    chunks = [(True, 0, first_size)]
    chunks += [(True, lo, CHUNK) for lo in range(first_size, prefix, CHUNK)]
    chunks += [(False, lo, min(CHUNK, span - lo)) for lo in range(0, span, CHUNK)]

    def pipeline_step(u):
        a_tile, a_pair = place(u)
        b_tile, b_pair = place(u - 1)
        c_tile, c_pair = place(u - 2)
        q_a = jnp.concatenate([v.T for v in heads_of(q_ref, a_pair, a_tile)], axis=1)
        q_c = jnp.concatenate(heads_of(q_ref, c_pair, c_tile), axis=0)
        b_top = jnp.max(top_ref[...], axis=0, keepdims=True)
        g_c = g_ref[...]
        delta_c = delta_ref[0:1]

        acc_p[:, dim:] += mm_nt(w_ref[top_rows], g_c)
        acc[window(c_tile), dim:] += mm_nt(w_ref[low_rows], g_c)

        tops = []
        for in_prefix, lo, size in chunks:
            at = pl.ds(lo if in_prefix else prefix + lo, size)
            if in_prefix:
                keys, values = pfx[pl.ds(lo, size), :dim], pfx[pl.ds(lo, size), dim:]
            else:
                keys = win[window(a_tile, lo, size), :dim]
                values = win[window(c_tile, lo, size), dim:]
            dp = mm(values, g_c) - delta_c
            d_ref[at] = (w_ref[at].astype(F32) * dp).astype(BF16)
            w_ref[at] = jnp.exp2((s_ref[at] - b_top) * step_scale).astype(BF16)
            score = mm(keys, q_a)
            if not in_prefix:
                score = score + jnp.concatenate([bias[pl.ds(lo, size)]] * PAIR, axis=1)
            s_ref[at] = score
            tops.append(jnp.max(score.reshape(-1, 8, width), axis=0))
        top_ref[...] = functools.reduce(jnp.maximum, tops)

        mixed = mm(pfx_vt[...], w_ref[top_rows])
        mixed = mixed + mm(win_vt[:, window(b_tile)], w_ref[low_rows])
        gq_t = mm(pfx_kt[...], d_ref[top_rows])
        gq_t = gq_t + mm(win_kt[:, window(c_tile)], d_ref[low_rows])
        acc_p[:, :dim] += mm(d_ref[top_rows], q_c)
        acc[window(c_tile), :dim] += mm(d_ref[low_rows], q_c)

        counted = jnp.where((slots_of(b_tile) < ends[-1]) & (u >= 1), F32(1), F32(0))
        inverse = jnp.concatenate([counted] * PAIR, axis=1) / mixed[dim : dim + 1]
        att_t = (mixed[:dim] * inverse).astype(BF16)
        up_t = jnp.concatenate([v.T for v in heads_of(up_ref, b_pair, b_tile)], axis=1)
        g_t = (up_t.astype(F32) * inverse).astype(BF16)
        g_ref[...] = g_t
        delta_ref[0:1] = jnp.sum(g_t.astype(F32) * att_t.astype(F32), axis=0, keepdims=True)
        put_heads(att, b_pair, b_tile, att_t)
        put_heads(gq, c_pair, c_tile, (gq_t * (factor2 * scale)).astype(BF16))

    def give_back(j):
        ret_out[part(j)] = acc[part(j)].astype(BF16)

        @pl.when(has_prev)
        def _():
            ret_copy(j).start()

    def loop_step(u, carry):
        @pl.when((lax.rem(u, pairs) == 0) & (u < units))
        def _():
            set_bias(place(u)[0])

        @pl.when(u == pairs)
        def _():
            for load in other_rows:
                load.wait()

            @pl.when(has_prev)
            def _():
                for j in order[1:]:
                    prev_copy(j).wait_recv()

            pl.loop(0, tiles - 1)(turn)

        for k in range(tiles - 1):

            @pl.when(u == (k + 1) * pairs + 2)
            def _():
                for copy in out_copies(order[k]):
                    copy.start()
                if k >= 1:
                    give_back(k - 1)

        pipeline_step(u)
        return carry

    lax.fori_loop(0, units + 2, loop_step, 0)

    for copy in out_copies(order[-1]):
        copy.start()
    gp_out[...] = acc_p[...].astype(BF16)
    for d, peer in enumerate(seq_peers):
        gp_copy(d, me, peer).start()
    for j in (tiles - 2, tiles - 1):
        give_back(j)

    final = jnp.concatenate([factor * scale, factor], axis=1)
    @pl.loop(0, tiles)
    def _(j):
        @pl.when(has_next)
        def _():
            pltpu.make_async_remote_copy(
                src_ref=ret_out.at[part(j)],
                dst_ref=ret_in.at[part(j)],
                send_sem=ret_send.at[j],
                recv_sem=ret_recv.at[j],
                device_id=(my_p, me + 1),
                device_id_type=pl.DeviceIdType.MESH,
            ).wait_recv()

        gkv[part(j)] = (acc[part(tiles + j)] + ret_in[part(j)].astype(F32)) * final
    gkv_copy = pltpu.make_async_copy(gkv, gkv_hbm.at[0], last_sem.at[0])
    gkv_copy.start()

    sums = acc_p[own_block]
    for d, peer in enumerate(seq_peers):
        gp_copy(d, peer, me).wait_recv()
        sums = sums + gp_in[peer].astype(F32)
    gpf[...] = sums * final
    gpf_copy = pltpu.make_async_copy(gpf, gpf_hbm.at[0], last_sem.at[1])
    gpf_copy.start()

    for d, peer in enumerate(seq_peers):
        pf_copy(d, me, peer).wait_send()
        gp_copy(d, me, peer).wait_send()
    for d, peer in enumerate(prompt_peers):
        len_copy(d, my_p, peer).wait_send()

    @pl.when(has_next)
    def _():
        for j in order:
            prev_copy(j).wait_send()

    @pl.when(has_prev)
    def _():
        for j in range(tiles):
            ret_copy(j).wait_send()

    for i in range(tiles):
        for copy in out_copies(i):
            copy.wait()
    gkv_copy.wait()
    gpf_copy.wait()


def body(n_prompt, n_seq, queries, resp_kv, prefix_kv, lengths, upstream):
    rows, width = queries.shape[1:]
    dim = resp_kv.shape[2] // 2
    block = prefix_kv.shape[1]
    prefix = block * n_seq
    tiles = rows // TILE
    keys = prefix + rows + TILE
    lanes = PAIR * dim
    pairs = width // lanes
    dma = pltpu.SemaphoreType.DMA
    anywhere = pl.BlockSpec(memory_space=pl.ANY)
    vmem = pltpu.VMEM
    out_shape = (
        jax.ShapeDtypeStruct(queries.shape, BF16),
        jax.ShapeDtypeStruct(queries.shape, BF16),
        jax.ShapeDtypeStruct(resp_kv.shape, F32),
        jax.ShapeDtypeStruct(prefix_kv.shape, F32),
    )
    placed = [
        pltpu.with_memory_space_constraint(x, pltpu.HBM)
        for x in (lengths, queries, resp_kv, prefix_kv, upstream)
    ]
    return pl.pallas_call(
        functools.partial(kernel, n_prompt, n_seq),
        out_shape=out_shape,
        in_specs=[pl.BlockSpec(memory_space=pltpu.SMEM)] + [pl.BlockSpec(memory_space=pltpu.HBM)] * 4,
        out_specs=(anywhere,) * 4,
        scratch_shapes=[
            vmem((pairs, rows, lanes), BF16),
            vmem((pairs, rows, lanes), BF16),
            vmem((2 * rows, 2 * dim), BF16),
            vmem((prefix, 2 * dim), BF16),
            vmem((dim, 2 * rows), BF16),
            vmem((dim + ONES, 2 * rows), BF16),
            vmem((dim, prefix), BF16),
            vmem((dim + ONES, prefix), BF16),
            vmem((rows + TILE, TILE), F32),
            vmem((keys, lanes), F32),
            vmem((8, lanes), F32),
            vmem((keys, lanes), BF16),
            vmem((dim, lanes), BF16),
            vmem((8, lanes), F32),
            vmem((keys, lanes), BF16),
            vmem((pairs, rows, lanes), BF16),
            vmem((pairs, rows, lanes), BF16),
            vmem((2 * rows, 2 * dim), F32),
            vmem((prefix, 2 * dim), F32),
            vmem((rows, 2 * dim), BF16),
            vmem((rows, 2 * dim), BF16),
            vmem((prefix, 2 * dim), BF16),
            vmem((n_seq, block, 2 * dim), BF16),
            vmem((rows, 2 * dim), F32),
            vmem((block, 2 * dim), F32),
            vmem((n_prompt, 8, 128), F32),
            dma((2,)),
            dma((2, pairs, 2)),
            dma((tiles, pairs, 2)),
            dma((2,)),
            dma((n_seq,)),
            dma((n_seq,)),
            dma((tiles,)),
            dma((tiles,)),
            dma((n_prompt,)),
            dma((n_prompt,)),
            dma((tiles,)),
            dma((tiles,)),
            dma((n_seq,)),
            dma((n_seq,)),
        ],
        compiler_params=pltpu.CompilerParams(
            collective_id=0, has_side_effects=True, vmem_limit_bytes=50 * 1024 * 1024
        ),
        name="attention_core",
    )(*placed)


def solution(mesh):
    spec = P("prompt", "seq", None)
    return jax.shard_map(
        functools.partial(body, mesh.shape["prompt"], mesh.shape["seq"]),
        mesh=mesh,
        in_specs=(spec, spec, spec, P("prompt", None), spec),
        out_specs=(spec, spec, spec, spec),
        check_vma=False,
    )
```
